512 devices in a mesh: dp: 16 (over y, core), tensor: 32 (over z, x).
Axes of the slice: x: 4, y: 8, z: 8, core: 2. Of those that a mesh axis runs over, the one named last changes fastest.
Arguments:
- x_in: bfloat16 [128, 128, 8192], P('dp', None, 'tensor'), may hold values from -16 to 16
- z_in: bfloat16 [128, 128, 8192], P('dp', None, 'tensor'), may hold values from -6 to 6
- b_in: bfloat16 [128, 128, 1024], P('dp'), may hold values from -1.5 to 1.5
- c_in: bfloat16 [128, 128, 1024], P('dp'), may hold values from -1.5 to 1.5
- dt_raw: float32 [128, 128, 128], P('dp', 'tensor'), may hold values from -4.2 to 5
- a_log: float32 [128], P('tensor'), may hold values from -3.52 to -0.91
- d_skip: float32 [128], P('tensor'), may hold values from 0.1 to 1.9
- norm_gain: float32 [8192], P('tensor'), may hold values from 0.1 to 1.9
- states: bfloat16 [128, 128, 64, 256], P('dp', 'tensor'), may hold values from -2 to 2
- dest: int32 [128], replicated, may hold values from 0 to 15, as said below
- accepted: int32 [128], replicated, may hold values from 1 to 128, as said below
Outputs:
- mixed: bfloat16 [128, 128, 8192], P('dp', None, 'tensor')
- new_states: bfloat16 [128, 128, 64, 256], P('dp', 'tensor')
The draws below stay inside these ranges and needn't reach their ends.
Inputs may be any that keep to these rules, and one draw needn't show every extreme that they name: `dest`: every group is the destination of exactly 8 tiles. One group sends at most 1 tile to one other group, and exactly 1 to some group. The offsets (destination minus source, modulo the number of groups) that a group uses form the same set for every group; where 8 allows, that set holds half the number of groups, then 1, then minus 1. `accepted`: tile 0 and some others accept all 128 rows.
All inputs are finite; a program needn't handle non-finite values.
Results may differ from the reference program's by a relative error of at most 0.011.
Values may be sent and summed in bfloat16 or wider, within the bound.
No kernel may reach another device: no remote copies, remote signals or barrier semaphores. Data moves between devices by JAX's collectives and lax.ppermute only.
A program may use at most 64 MiB of HBM per device.

```python
import jax
import jax.numpy as jnp
from jax import lax

HEADS = 128
HEAD_DIM = 64
STATE = 256
GROUPS = 4
BLOCK_HEIGHT = 128
TILES_DEV = 8
BLOCK_COUNT = 128
CHANNELS = 8192


def draw_x_in(key, part):
    key = jax.random.fold_in(key, 11)
    key_cols, key_rows, seed_stream = jax.random.split(key, 3)
    shape = (BLOCK_COUNT, BLOCK_HEIGHT, CHANNELS)
    where_col = jnp.arange(CHANNELS, dtype=jnp.float32) / max(CHANNELS - 1, 1)
    col_noise = jax.random.uniform(key_cols, (CHANNELS,), jnp.float32)
    col_scale = 10.0 ** (0.5 * where_col + 0.5 * col_noise - 0.5)
    row_scale = 10.0 ** (0.5 * jax.random.uniform(key_rows, (BLOCK_COUNT, BLOCK_HEIGHT, 1), jnp.float32) - 0.25)
    starting_position = jax.random.normal(seed_stream, shape, jnp.float32)
    return jnp.clip(starting_position * col_scale * row_scale, -16.0, 16.0).astype(jnp.bfloat16)


def draw_a_log(key, part):
    key = jax.random.fold_in(key, 12)
    key_fast, key_rate = jax.random.split(key)
    share = 0.5
    fast = jax.random.uniform(key_fast, (HEADS,), jnp.float32) < share
    spread = jax.random.uniform(key_rate, (HEADS,), jnp.float32)
    rate = jnp.where(fast, 0.25 * 1.6 ** spread, 0.03 * 3.3 ** spread)
    return jnp.log(rate).astype(jnp.float32)


def draw_dt_raw(key, part):
    key = jax.random.fold_in(key, 13)
    seed_stream, spell_seed_stream = jax.random.split(key)
    shape = (BLOCK_COUNT, HEADS, BLOCK_HEIGHT)
    starting_position = -2.2 + jnp.clip(0.5 * jax.random.normal(seed_stream, shape, jnp.float32), -2.0, 2.0)
    span_extent = jax.random.uniform(spell_seed_stream, (BLOCK_COUNT, 1, BLOCK_HEIGHT), jnp.float32) < 2.0 / BLOCK_HEIGHT
    return jnp.where(span_extent, 5.0, starting_position).astype(jnp.float32)


def draw_dest(key, part):
    key = jax.random.fold_in(key, 14)
    key_offsets, key_orders = jax.random.split(key)
    group_count = BLOCK_COUNT // TILES_DEV
    values = jnp.arange(group_count, dtype=jnp.int32)
    random_rank = jax.random.permutation(key_offsets, group_count).astype(jnp.int32)
    score = jnp.where(values == group_count // 2, -3, jnp.where(values == 1 % group_count, -2, jnp.where(values == group_count - 1, -1, random_rank)))
    offsets = jnp.argsort(score, stable=True).astype(jnp.int32)
    order_keys = jax.random.split(key_orders, group_count)
    orders = jax.vmap(lambda one_key: jax.random.permutation(one_key, TILES_DEV))(order_keys)
    sources = jnp.arange(group_count, dtype=jnp.int32)[:, None]
    targets = (sources + offsets[orders % group_count]) % group_count
    return targets.reshape(-1).astype(jnp.int32)


def draw_accepted(key, part):
    key = jax.random.fold_in(key, 15)
    key_full, key_count = jax.random.split(key)
    full = jax.random.randint(key_full, (BLOCK_COUNT,), 0, 2) == 0
    counts = jax.random.randint(key_count, (BLOCK_COUNT,), 1, BLOCK_HEIGHT + 1)
    chosen = jnp.where(full, BLOCK_HEIGHT, counts)
    return chosen.at[0].set(BLOCK_HEIGHT).astype(jnp.int32)


def block_scale(key, extent, pieces, smallest, high):
    loudness = 1.0
    for position, parts in pieces:
        draws = jax.random.uniform(jax.random.fold_in(jax.random.fold_in(key, 6), position), (parts,), jnp.float32, smallest / len(pieces), high / len(pieces))
        loudness = loudness * jnp.repeat(jnp.exp(draws), extent[position] // parts).reshape((-1,) + (1,) * (len(extent) - 1 - position))
    return loudness


def noise(stream_key, shape, deviation, bound, shards=(), kind=jnp.bfloat16):
    factor_of = block_scale(stream_key, shape, shards, -0.22, 0.18) if shards else 1.0
    array = jax.random.normal(stream_key, shape, jnp.float32) * deviation * factor_of
    return jnp.minimum(jnp.maximum(array, -bound), bound).astype(kind)


def setup_inputs(seed: int = 0) -> dict:
    key_of = jax.random.split(jax.random.key(seed), 12)
    return {
        "x_in": draw_x_in(jax.random.fold_in(key_of[11], 71), 0),
        "z_in": noise(key_of[1], (BLOCK_COUNT, BLOCK_HEIGHT, CHANNELS), 1.0, 6.0, ((0, 16), (2, 32))),
        "b_in": noise(key_of[2], (BLOCK_COUNT, BLOCK_HEIGHT, GROUPS * STATE), 0.25, 1.5, ((0, 16),)),
        "c_in": noise(key_of[3], (BLOCK_COUNT, BLOCK_HEIGHT, GROUPS * STATE), 0.25, 1.5, ((0, 16),)),
        "dt_raw": draw_dt_raw(jax.random.fold_in(key_of[11], 71), 0),
        "a_log": draw_a_log(jax.random.fold_in(key_of[11], 71), 0),
        "d_skip": jnp.clip(1.0 + 0.18 * jax.random.normal(key_of[6], (HEADS,), jnp.float32), 0.1, 1.9),
        "norm_gain": jnp.clip(1.0 + 0.18 * jax.random.normal(key_of[7], (CHANNELS,), jnp.float32), 0.1, 1.9),
        "states": noise(key_of[8], (BLOCK_COUNT, HEADS, HEAD_DIM, STATE), 0.3, 2.0, ((0, 16), (1, 32))),
        "dest": draw_dest(jax.random.fold_in(key_of[11], 71), 0),
        "accepted": draw_accepted(jax.random.fold_in(key_of[11], 71), 0),
    }


def block_arithmetic(x_in, b_in, c_in, dt_raw, a_log, d_skip, prefix, accepted):
    tile_count, row_count, channels = x_in.shape
    head_count = dt_raw.shape[1]
    state_width = prefix.shape[-1]
    head_width = channels // head_count
    group_count = b_in.shape[2] // state_width
    tiles_per_group = head_count // group_count
    b_groups = b_in.astype(jnp.float32).reshape(tile_count, row_count, group_count, state_width)
    c_groups = c_in.astype(jnp.float32).reshape(tile_count, row_count, group_count, state_width)
    step_size = jax.nn.softplus(dt_raw)
    cumulative = jnp.cumsum(-jnp.exp(a_log)[None, :, None] * step_size, axis=2)
    row_ids = lax.broadcasted_iota(jnp.int32, (row_count, row_count), 0)
    col_ids = lax.broadcasted_iota(jnp.int32, (row_count, row_count), 1)
    lower = col_ids <= row_ids
    spread = cumulative[:, :, :, None] - cumulative[:, :, None, :]
    decay = jnp.where(lower, jnp.exp(jnp.where(lower, spread, 0.0)), 0.0)
    products = jnp.einsum('slgn,smgn->sglm', c_groups, b_groups)
    shaped = (tile_count, group_count, tiles_per_group, row_count, row_count)
    weights = (products[:, :, None] * decay.reshape(shaped) * step_size.reshape(tile_count, group_count, tiles_per_group, 1, row_count)).astype(jnp.bfloat16)
    x_groups = x_in.reshape(tile_count, row_count, group_count, tiles_per_group, head_width)
    within = jnp.einsum('sghlm,smghp->slghp', weights.astype(jnp.float32), x_groups.astype(jnp.float32))
    prefix_groups = prefix.reshape(tile_count, group_count, tiles_per_group, head_width, state_width)
    carried = jnp.einsum('slgn,sghpn->slghp', c_groups, prefix_groups.astype(jnp.float32))
    fading = jnp.exp(cumulative).reshape(tile_count, group_count, tiles_per_group, row_count).transpose(0, 3, 1, 2)[..., None]
    skip = d_skip.reshape(group_count, tiles_per_group)[None, None, :, :, None] * x_groups.astype(jnp.float32)
    ssm_out = (within + fading * carried + skip).reshape(tile_count, row_count, channels).astype(jnp.bfloat16)
    positions = lax.broadcasted_iota(jnp.int32, (tile_count, row_count), 1)
    last_row = positions == accepted[:, None] - 1
    kept = positions < accepted[:, None]
    final = lax.optimization_barrier(jnp.sum(jnp.where(last_row[:, None, :], cumulative, 0.0), axis=2))
    gap = jnp.where(kept[:, None, :], final[:, :, None] - cumulative, 0.0)
    scale = jnp.where(kept[:, None, :], jnp.exp(gap), 0.0) * step_size
    scale_rows = scale.reshape(tile_count, group_count, tiles_per_group, row_count).transpose(0, 3, 1, 2)[..., None]
    inputs_kept = (x_groups.astype(jnp.float32) * scale_rows).astype(jnp.bfloat16)
    added = jnp.einsum('slghp,slgn->sghpn', inputs_kept.astype(jnp.float32), b_groups)
    fade_end = jnp.exp(final).reshape(tile_count, group_count, tiles_per_group)[..., None, None]
    new_state = fade_end * prefix_groups.astype(jnp.float32) + added
    return (ssm_out, new_state.reshape(prefix.shape).astype(jnp.bfloat16))

def reference(x_in, z_in, b_in, c_in, dt_raw, a_log, d_skip, norm_gain, states, dest, accepted):
    tile_count = dest.shape[0]
    tile_index = jnp.arange(tile_count, dtype=jnp.int32)
    same_dest = dest[:, None] == dest[None, :]
    before = tile_index[None, :] < tile_index[:, None]
    slot_ids = (TILES_DEV * dest + lax.optimization_barrier(jnp.sum(same_dest & before, axis=1))).astype(jnp.int32)

    def one_tile(items):
        x_tile, z_tile, b_tile, c_tile, dt_tile, slot_id, accept = items
        prefix = lax.dynamic_index_in_dim(states, slot_id, 0, keepdims=True)
        ssm_out, state = block_arithmetic(x_tile[None], b_tile[None], c_tile[None], dt_tile[None], a_log, d_skip, prefix, accept[None])
        gated = ssm_out[0].astype(jnp.float32) * jax.nn.silu(z_tile.astype(jnp.float32))
        row_count = gated.shape[0]
        grouped = gated.reshape(row_count, GROUPS, CHANNELS // GROUPS)
        square_mean = lax.optimization_barrier(jnp.mean(grouped * grouped, axis=-1, keepdims=True))
        rescaled_vector = (grouped * lax.rsqrt(square_mean + 1e-05)).reshape(row_count, CHANNELS)
        mixed = (rescaled_vector * norm_gain).astype(jnp.bfloat16)
        return (mixed, state[0])
    mixed, fresh = lax.map(one_tile, (x_in, z_in, b_in, c_in, dt_raw, slot_ids, accepted))
    new_states = jnp.zeros_like(states).at[slot_ids].set(fresh)
    return (mixed, new_states)
```

```python
import jax
import jax.numpy as jnp
from jax import lax
from jax.sharding import PartitionSpec as P

GROUPS = 4
CHANNELS = 8192


def block_arithmetic(x_in, b_in, c_in, dt_raw, a_log, d_skip, prefix, accepted):
    tile_count, row_count, channels = x_in.shape
    head_count = dt_raw.shape[1]
    state_width = prefix.shape[-1]
    head_width = channels // head_count
    group_count = b_in.shape[2] // state_width
    tiles_per_group = head_count // group_count
    b_groups = b_in.reshape(tile_count, row_count, group_count, state_width)
    c_groups = c_in.reshape(tile_count, row_count, group_count, state_width)
    step_size = jax.nn.softplus(dt_raw)
    cumulative = jnp.cumsum(-jnp.exp(a_log)[None, :, None] * step_size, axis=2)
    row_ids = lax.broadcasted_iota(jnp.int32, (row_count, row_count), 0)
    col_ids = lax.broadcasted_iota(jnp.int32, (row_count, row_count), 1)
    lower = col_ids <= row_ids
    spread = cumulative[:, :, :, None] - cumulative[:, :, None, :]
    decay = jnp.where(lower, jnp.exp(jnp.where(lower, spread, 0.0)), 0.0)
    products = jnp.einsum("slgn,smgn->sglm", c_groups, b_groups, preferred_element_type=jnp.float32)
    shaped = (tile_count, group_count, tiles_per_group, row_count, row_count)
    weights = (
        products[:, :, None]
        * decay.reshape(shaped)
        * step_size.reshape(tile_count, group_count, tiles_per_group, 1, row_count)
    ).astype(jnp.bfloat16)
    x_groups = x_in.reshape(tile_count, row_count, group_count, tiles_per_group, head_width)
    within = jnp.einsum("sghlm,smghp->slghp", weights, x_groups, preferred_element_type=jnp.float32)
    prefix_groups = prefix.reshape(
        tile_count, group_count, tiles_per_group, head_width, state_width
    )
    carried = jnp.einsum(
        "slgn,sghpn->slghp", c_groups, prefix_groups, preferred_element_type=jnp.float32
    )
    fading = (
        jnp.exp(cumulative)
        .reshape(tile_count, group_count, tiles_per_group, row_count)
        .transpose(0, 3, 1, 2)[..., None]
    )
    skip = d_skip.reshape(group_count, tiles_per_group)[None, None, :, :, None] * x_groups.astype(
        jnp.float32
    )
    ssm_out = (
        (within + fading * carried + skip)
        .reshape(tile_count, row_count, channels)
        .astype(jnp.bfloat16)
    )
    positions = lax.broadcasted_iota(jnp.int32, (tile_count, row_count), 1)
    last_row = positions == accepted[:, None] - 1
    kept = positions < accepted[:, None]
    final = jnp.sum(jnp.where(last_row[:, None, :], cumulative, 0.0), axis=2)
    gap = jnp.where(kept[:, None, :], final[:, :, None] - cumulative, 0.0)
    scale = jnp.where(kept[:, None, :], jnp.exp(gap), 0.0) * step_size
    scale_rows = scale.reshape(tile_count, group_count, tiles_per_group, row_count).transpose(
        0, 3, 1, 2
    )[..., None]
    inputs_kept = (x_groups.astype(jnp.float32) * scale_rows).astype(jnp.bfloat16)
    added = jnp.einsum(
        "slghp,slgn->sghpn", inputs_kept, b_groups, preferred_element_type=jnp.float32
    )
    fade_end = jnp.exp(final).reshape(tile_count, group_count, tiles_per_group)[..., None, None]
    new_state = fade_end * prefix_groups.astype(jnp.float32) + added
    return (ssm_out, new_state.reshape(prefix.shape).astype(jnp.bfloat16))


def routing(dest, own_group, group_count, tiles_dev, capacity):
    dest_table = dest.reshape(group_count, tiles_dev)
    tile_index = jnp.arange(tiles_dev, dtype=jnp.int32)
    same_dest = dest_table[:, :, None] == dest_table[:, None, :]
    before = tile_index[None, :] < tile_index[:, None]
    order_rank = jnp.sum(same_dest & before[None], axis=2)
    slot_place = dest_table * capacity + order_rank
    own_slots = jnp.take(slot_place, own_group, axis=0)
    slot_ids = jnp.arange(group_count * capacity, dtype=jnp.int32)
    sender = jnp.sum(
        jnp.where(own_slots[None, :] == slot_ids[:, None], tile_index[None, :], 0), axis=1
    )
    slot_turn = jnp.arange(capacity, dtype=jnp.int32)
    matched = (dest_table[:, None, :] == own_group) & (
        order_rank[:, None, :] == slot_turn[None, :, None]
    )
    is_live = jnp.any(matched, axis=2).reshape(-1)
    local_tile = jnp.sum(jnp.where(matched, tile_index[None, None, :], 0), axis=2)
    source_tile = (
        jnp.arange(group_count, dtype=jnp.int32)[:, None] * tiles_dev + local_tile
    ).reshape(-1)
    counted = is_live.astype(jnp.int32)
    compact_slot = jnp.cumsum(counted) - counted
    inverse = jnp.sum(
        jnp.where(
            is_live[None, :] & (compact_slot[None, :] == tile_index[:, None]), slot_ids[None, :], 0
        ),
        axis=1,
    )
    compact_slot = jnp.where(is_live, compact_slot, 0)
    return (own_slots, sender, source_tile, inverse, compact_slot)


def on_device(x_in, z_in, b_in, c_in, dt_raw, a_log, d_skip, norm_gain, states, dest, accepted):
    group_count = lax.axis_size("dp")
    tiles_dev = x_in.shape[0]
    capacity = (tiles_dev + group_count - 1) // group_count
    own_group = lax.axis_index("dp")
    state_width = states.shape[-1]
    head_group = lax.axis_index("tensor") // (lax.axis_size("tensor") // GROUPS)
    b_mine = lax.dynamic_slice_in_dim(b_in, head_group * state_width, state_width, 2)
    c_mine = lax.dynamic_slice_in_dim(c_in, head_group * state_width, state_width, 2)
    own_slots, sender, source_tile, inverse, compact_slot = routing(
        dest, own_group, group_count, tiles_dev, capacity
    )
    x_send = jnp.take(x_in, sender, axis=0)
    b_send = jnp.take(b_mine, sender, axis=0)
    c_send = jnp.take(c_mine, sender, axis=0)
    dt_send = jnp.take(dt_raw, sender, axis=0)
    x_got, b_got, c_got, dt_got = (
        lax.all_to_all(x_send, "dp", split_axis=0, concat_axis=0, tiled=True),
        lax.all_to_all(b_send, "dp", split_axis=0, concat_axis=0, tiled=True),
        lax.all_to_all(c_send, "dp", split_axis=0, concat_axis=0, tiled=True),
        lax.all_to_all(
            dt_send.astype(jnp.bfloat16), "dp", split_axis=0, concat_axis=0, tiled=True
        ).astype(dt_send.dtype),
    )
    accept_here = jnp.take(accepted, jnp.take(source_tile, inverse, axis=0), axis=0)
    ssm_here, new_states = block_arithmetic(
        jnp.take(x_got, inverse, axis=0),
        jnp.take(b_got, inverse, axis=0),
        jnp.take(c_got, inverse, axis=0),
        jnp.take(dt_got, inverse, axis=0),
        a_log,
        d_skip,
        states,
        accept_here,
    )
    returned = lax.all_to_all(
        jnp.take(ssm_here, compact_slot, axis=0), "dp", split_axis=0, concat_axis=0, tiled=True
    )
    ssm_out = jnp.take(returned, own_slots, axis=0)
    gated = ssm_out.astype(jnp.float32) * jax.nn.silu(z_in.astype(jnp.float32))
    local_squares = jnp.sum(gated * gated, axis=-1)
    tensor_count = lax.axis_size("tensor")
    group_size = tensor_count // GROUPS
    group_members = [list(range(g * group_size, (g + 1) * group_size)) for g in range(GROUPS)]
    copies = jnp.broadcast_to(local_squares[None], (group_size,) + local_squares.shape)
    gathered = lax.all_to_all(
        copies, "tensor", split_axis=0, concat_axis=0, axis_index_groups=group_members, tiled=True
    )
    group_total = jnp.sum(gathered, axis=0)
    factor = lax.rsqrt(group_total / (CHANNELS // GROUPS) + 1e-05)
    mixed = (gated * factor[:, :, None] * norm_gain).astype(jnp.bfloat16)
    return (mixed, new_states)


def solution(mesh):
    in_specs = (
        P("dp", None, "tensor"),
        P("dp", None, "tensor"),
        P("dp", None, None),
        P("dp", None, None),
        P("dp", "tensor", None),
        P("tensor"),
        P("tensor"),
        P("tensor"),
        P("dp", "tensor", None, None),
        P(),
        P(),
    )
    out_specs = (P("dp", None, "tensor"), P("dp", "tensor", None, None))
    return jax.shard_map(
        on_device, mesh=mesh, in_specs=in_specs, out_specs=out_specs, check_vma=False
    )
```

```python
import functools
import itertools

import jax
import jax.numpy as jnp
from jax import lax
from jax.experimental import pallas as pl
from jax.experimental.pallas import tpu as pltpu
from jax.sharding import PartitionSpec as P

GROUPS = 4
TILES = 8
HEADS_DEV = 4
HEAD_DIM = 64
STATE = 256
ROWS = 128
WIDTH = HEADS_DEV * HEAD_DIM
MESSAGE = WIDTH + 16
FIXED = (1, 15, 8)
PAIRS = ((2, 4, 6), (3, 5, 7))
SIDES = tuple(v for part in PAIRS for k in part for v in (k, 16 - k))
VMEM_BYTES = 24 * 1024 * 1024
F32 = jnp.float32
BF16 = jnp.bfloat16
ANY = pl.BlockSpec(memory_space=pl.ANY)
NT = (((1,), (1,)), ((), ()))
TN = (((0,), (0,)), ((), ()))


def params():
    return pltpu.CompilerParams(vmem_limit_bytes=VMEM_BYTES)


def whole(shape):
    return pl.BlockSpec(shape, lambda *_: (0,) * len(shape))


def of_group(shape):
    return pl.BlockSpec(shape, lambda i, info: (0, 0, info[0]))


def lane_ids(shape):
    return lax.broadcasted_iota(jnp.int32, shape, len(shape) - 1)


def step_rows(dt_ref, a_ref, rows_ref):
    for t in range(TILES):
        rows_ref[pl.ds(t * HEADS_DEV, HEADS_DEV), :] = dt_ref[t]
    raw = rows_ref[...]
    step = jnp.maximum(raw, 0.0) + jnp.log1p(jnp.exp(-jnp.abs(raw)))
    for t in range(TILES):
        rows_ref[pl.ds(t * HEADS_DEV, HEADS_DEV), :] = jnp.broadcast_to(
            a_ref[...], (HEADS_DEV, ROWS)
        )
    total = -jnp.exp(rows_ref[...]) * step
    lanes = lane_ids(total.shape)
    shift = 1
    while shift < ROWS:
        total = total + jnp.where(lanes >= shift, pltpu.roll(total, shift, 1), 0.0)
        shift *= 2
    return step, total


def spread_heads(columns, t):
    low = lane_ids((ROWS, 2 * HEAD_DIM)) < HEAD_DIM
    halves = []
    for j in range(2):
        at = t * HEADS_DEV + 2 * j
        halves.append(jnp.where(low, columns[:, at : at + 1], columns[:, at + 1 : at + 2]))
    return jnp.concatenate(halves, axis=1)


def added_kernel(info_ref, x_ref, b_ref, dt_ref, a_ref, states_ref, send_ref, rows_ref):
    step, total = step_rows(dt_ref, a_ref, rows_ref)
    shape = total.shape
    lanes = lane_ids(shape)
    row_tile = lax.broadcasted_iota(jnp.int32, shape, 0) // HEADS_DEV
    accepted = jnp.zeros(shape, jnp.int32)
    for t in range(TILES):
        accepted = jnp.where(row_tile == t, info_ref[1 + t], accepted)
    final = jnp.sum(jnp.where(lanes == accepted - 1, total, 0.0), axis=1, keepdims=True)
    kept = lanes < accepted
    scale = jnp.where(kept, jnp.exp(jnp.where(kept, final - total, 0.0)), 0.0) * step
    columns = jnp.transpose(scale)
    fade = jnp.broadcast_to(jnp.exp(final), (shape[0], STATE))
    fade_high = fade.astype(BF16).astype(F32)
    fade_low = fade - fade_high
    empty = jnp.zeros((8, STATE), F32)
    for t in range(TILES):
        x_kept = (x_ref[t].astype(F32) * spread_heads(columns, t)).astype(BF16)
        added = lax.dot_general(x_kept, b_ref[t], TN, preferred_element_type=F32)
        send_ref[t, pl.ds(0, WIDTH), :] = added.astype(BF16)
        at = t * HEADS_DEV
        tail = jnp.concatenate(
            [fade_high[at : at + HEADS_DEV], fade_low[at : at + HEADS_DEV], empty], axis=0
        )
        send_ref[t, pl.ds(WIDTH, 16), :] = tail.astype(BF16)
        send_ref[TILES + t, pl.ds(0, WIDTH), :] = states_ref[t]
        send_ref[TILES + t, pl.ds(WIDTH, 16), :] = jnp.zeros((16, STATE), BF16)


def within_kernel(info_ref, x_ref, b_ref, c_ref, dt_ref, a_ref, d_ref, out_ref, fade_ref, rows_ref):
    step, total = step_rows(dt_ref, a_ref, rows_ref)
    columns = jnp.transpose(total)
    fade_ref[...] = jnp.exp(columns)
    lower = lane_ids((ROWS, ROWS)) <= lax.broadcasted_iota(jnp.int32, (ROWS, ROWS), 0)
    wide = lane_ids((ROWS, WIDTH)) // HEAD_DIM
    for t in range(TILES):
        products = lax.dot_general(c_ref[t], b_ref[t], NT, preferred_element_type=F32)
        x = x_ref[t]
        weights = []
        inputs = []
        for h in range(HEADS_DEV):
            at = t * HEADS_DEV + h
            gap = columns[:, at : at + 1] - total[at : at + 1, :]
            decay = jnp.exp(jnp.where(lower, gap, -1e30))
            weights.append((products * decay * step[at : at + 1, :]).astype(BF16))
            inputs.append(jnp.where(wide == h, x, jnp.zeros_like(x)))
        within = lax.dot_general(
            jnp.concatenate(weights, axis=1),
            jnp.concatenate(inputs, axis=0),
            (((1,), (0,)), ((), ())),
            preferred_element_type=F32,
        )
        out_ref[t] = within + d_ref[...] * x.astype(F32)


def fetch(table_ref, sources, held_ref, sems):
    for i, source in enumerate(sources):
        slot = table_ref[i]

        @pl.when(slot >= 0)
        def _():
            pltpu.make_async_copy(source(), held_ref.at[slot], sems.at[slot]).start()


def gate_kernel(table_ref, info_ref, c_ref, z_ref, within_ref, fade_ref, *rest):
    refs, (gated_ref, squares_ref, held_ref, sems) = rest[:-4], rest[-4:]
    states, fixed, first, second = refs[0], refs[1:4], refs[4:16], refs[16:]
    part = pl.ds(0, WIDTH)
    sources = [lambda: states.at[table_ref[28]]]
    sources += [lambda ref=ref: ref.at[1, part, :] for ref in fixed]
    sources += [lambda ref=ref: ref.at[part, :] for ref in first + second]
    fetch(table_ref, sources, held_ref, sems)
    columns = fade_ref[...]
    lanes = lane_ids((ROWS, ROWS))
    squares = jnp.zeros((ROWS, ROWS), F32)
    for t in range(TILES):
        pltpu.make_async_copy(states.at[0], held_ref.at[t], sems.at[t]).wait()
        carried = lax.dot_general(c_ref[t], held_ref[t], NT, preferred_element_type=F32)
        total = within_ref[t] + spread_heads(columns, t) * carried
        z = z_ref[t].astype(F32)
        gated = total.astype(BF16).astype(F32) * (z / (1.0 + jnp.exp(-z)))
        gated_ref[t] = gated
        squares = jnp.where(lanes == t, jnp.sum(gated * gated, axis=1, keepdims=True), squares)
    turned = jnp.transpose(squares)[:TILES]
    for i in range(squares_ref.shape[0]):
        squares_ref[i] = turned


def norm_kernel(gated_ref, squares_ref, gain_ref, out_ref):
    total = jnp.sum(squares_ref[...], axis=0)
    factor = lax.rsqrt(total / (GROUPS_WIDTH) + 1e-05)
    filled = jnp.concatenate([factor, jnp.zeros((ROWS - TILES, ROWS), F32)], axis=0)
    columns = jnp.transpose(filled)
    gain = gain_ref[...]
    for t in range(TILES):
        out_ref[t] = (gated_ref[t] * columns[:, t : t + 1] * gain).astype(BF16)


GROUPS_WIDTH = 2048.0


def state_kernel(table_ref, states_ref, *rest):
    refs, (out_ref, held_ref, sems) = rest[:-3], rest[-3:]
    send, fixed, first = refs[0], refs[1:4], refs[4:]
    sources = [lambda: send.at[table_ref[28]]]
    sources += [lambda ref=ref: ref.at[0] for ref in fixed]
    sources += [lambda ref=ref: ref for ref in first]
    fetch(table_ref, sources, held_ref, sems)
    for t in range(TILES):
        pltpu.make_async_copy(send.at[0], held_ref.at[t], sems.at[t]).wait()
        tail = held_ref[t, pl.ds(WIDTH, 16), :].astype(F32)
        for h in range(HEADS_DEV):
            rows = pl.ds(h * HEAD_DIM, HEAD_DIM)
            fade = tail[h : h + 1] + tail[HEADS_DEV + h : HEADS_DEV + h + 1]
            out_ref[t, rows, :] = (
                fade * states_ref[t, rows, :].astype(F32) + held_ref[t, rows, :].astype(F32)
            ).astype(BF16)


def shifted(message, offset):
    count = lax.axis_size("dp")
    return lax.ppermute(message, "dp", [(i, (i + offset) % count) for i in range(count)])


def pick(messages, index):
    return lax.dynamic_index_in_dim(messages, index, 0, keepdims=False)


def exchange(part, kinds, messages, one, added_at, prefix_at):
    first, second = [], []
    blank = jnp.zeros((MESSAGE, STATE), BF16)
    for k, kind in zip(part, kinds):
        for v in (k, 16 - k):
            if kind == 0:
                first.append(blank)
                second.append(blank)
            elif kind == 1:
                first.append(shifted(pick(messages, one[v]), v))
                second.append(blank)
            else:
                both = jnp.stack([pick(messages, added_at[v]), pick(messages, prefix_at[v])])
                got = shifted(both, v)
                first.append(got[0])
                second.append(got[1])
    return tuple(first), tuple(second)


def on_device(x_in, z_in, b_in, c_in, dt_raw, a_log, d_skip, norm_gain, states, dest, accepted):
    count = lax.axis_size("dp")
    me = lax.axis_index("dp")
    tensor_count = lax.axis_size("tensor")
    group_size = tensor_count // GROUPS
    head_group = lax.axis_index("tensor") // group_size

    offsets = jnp.arange(count, dtype=jnp.int32)
    turn = jnp.arange(TILES, dtype=jnp.int32)
    dest_table = dest.reshape(count, TILES)
    used = jnp.any(dest_table[0][None, :] == offsets[:, None], axis=1)
    own = lax.dynamic_index_in_dim(dest_table, me, 0, keepdims=False)
    own_offset = (own - me) % count
    sender = jnp.sum(
        jnp.where(own_offset[None, :] == offsets[:, None], turn[None, :], 0), axis=1
    ).astype(jnp.int32)
    source = (me - offsets) % count
    rank = jnp.sum(
        (source[None, :] < source[:, None]) & used[None, :], axis=1, dtype=jnp.int32
    )
    against = (count - offsets) % count
    used_against = jnp.take(used, against)
    sender_against = jnp.take(sender, against)
    prefix_at = TILES + jnp.take(rank, against)
    one = jnp.where(used, sender, prefix_at)
    kind = used.astype(jnp.int32) + used_against.astype(jnp.int32)

    fixed_v = jnp.array(FIXED, jnp.int32)
    side_v = jnp.array(SIDES, jnp.int32)
    side_kind = kind[side_v]
    none = jnp.int32(-1)
    prefix_table = jnp.concatenate(
        [
            jnp.where(used[0], sender[0], none)[None],
            sender_against[fixed_v],
            jnp.where((side_kind == 1) & used_against[side_v], sender_against[side_v], none),
            jnp.where(side_kind == 2, sender_against[side_v], none),
            rank[0][None],
        ]
    ).astype(jnp.int32)
    added_table = jnp.concatenate(
        [
            jnp.where(used[0], rank[0], none)[None],
            rank[fixed_v],
            jnp.where(used[side_v], rank[side_v], none),
            jnp.full((12,), -1, jnp.int32),
            sender[0][None],
        ]
    ).astype(jnp.int32)
    accept_mine = lax.dynamic_slice_in_dim(accepted, me * TILES, TILES, 0)
    info = jnp.concatenate([head_group[None], accept_mine]).astype(jnp.int32)

    a_column = a_log.reshape(HEADS_DEV, 1)
    d_row = jnp.repeat(d_skip, HEAD_DIM).reshape(1, WIDTH)
    gain_row = norm_gain.reshape(1, WIDTH)
    state_rows = states.reshape(TILES, WIDTH, STATE)
    tile_shape = (TILES, ROWS, WIDTH)
    dt_shape = dt_raw.shape
    rows_scratch = pltpu.VMEM((TILES * HEADS_DEV, ROWS), F32)

    messages = pl.pallas_call(
        added_kernel,
        grid_spec=pltpu.PrefetchScalarGridSpec(
            num_scalar_prefetch=1,
            grid=(1,),
            in_specs=[
                whole(tile_shape),
                of_group((TILES, ROWS, STATE)),
                whole(dt_shape),
                whole(a_column.shape),
                whole(state_rows.shape),
            ],
            out_specs=whole((2 * TILES, MESSAGE, STATE)),
            scratch_shapes=[rows_scratch],
        ),
        out_shape=jax.ShapeDtypeStruct((2 * TILES, MESSAGE, STATE), BF16),
        compiler_params=params(),
        name="added",
    )(info, x_in, b_in, dt_raw, a_column, state_rows)

    fixed = []
    for v in FIXED:
        both = jnp.stack([pick(messages, sender[v]), pick(messages, prefix_at[v])])
        fixed.append(shifted(both, v))

    within, fade = pl.pallas_call(
        within_kernel,
        grid_spec=pltpu.PrefetchScalarGridSpec(
            num_scalar_prefetch=1,
            grid=(1,),
            in_specs=[
                whole(tile_shape),
                of_group((TILES, ROWS, STATE)),
                of_group((TILES, ROWS, STATE)),
                whole(dt_shape),
                whole(a_column.shape),
                whole(d_row.shape),
            ],
            out_specs=[whole(tile_shape), whole((ROWS, TILES * HEADS_DEV))],
            scratch_shapes=[rows_scratch],
        ),
        out_shape=[
            jax.ShapeDtypeStruct(tile_shape, F32),
            jax.ShapeDtypeStruct((ROWS, TILES * HEADS_DEV), F32),
        ],
        compiler_params=params(),
        name="within",
    )(info, x_in, b_in, c_in, dt_raw, a_column, d_row)

    first, second = (), ()
    sent = messages
    for part in PAIRS:
        code = jnp.int32(0)
        branches = []
        for k in part:
            code = code * 3 + kind[k]
        for kinds in itertools.product(range(3), repeat=len(part)):
            branches.append(functools.partial(exchange, part, kinds))
        more_first, more_second = lax.switch(code, branches, sent, one, sender, prefix_at)
        first, second = first + more_first, second + more_second

    gated, squares = pl.pallas_call(
        gate_kernel,
        grid_spec=pltpu.PrefetchScalarGridSpec(
            num_scalar_prefetch=2,
            grid=(1,),
            in_specs=[
                pl.BlockSpec((TILES, ROWS, STATE), lambda i, table, info: (0, 0, info[0])),
                whole(tile_shape),
                whole(tile_shape),
                whole(fade.shape),
            ]
            + [ANY] * 28,
            out_specs=[whole(tile_shape), whole((group_size, TILES, ROWS))],
            scratch_shapes=[
                pltpu.VMEM((TILES, WIDTH, STATE), BF16),
                pltpu.SemaphoreType.DMA((TILES,)),
            ],
        ),
        out_shape=[
            jax.ShapeDtypeStruct(tile_shape, F32),
            jax.ShapeDtypeStruct((group_size, TILES, ROWS), F32),
        ],
        compiler_params=params(),
        name="gate",
    )(prefix_table, info, c_in, z_in, within, fade, state_rows, *fixed, *first, *second)

    members = [list(range(g * group_size, (g + 1) * group_size)) for g in range(GROUPS)]
    all_squares = lax.all_to_all(
        squares, "tensor", split_axis=0, concat_axis=0, axis_index_groups=members, tiled=True
    )

    new_states = pl.pallas_call(
        state_kernel,
        grid_spec=pltpu.PrefetchScalarGridSpec(
            num_scalar_prefetch=1,
            grid=(1,),
            in_specs=[whole(state_rows.shape)] + [ANY] * 16,
            out_specs=whole(state_rows.shape),
            scratch_shapes=[
                pltpu.VMEM((TILES, MESSAGE, STATE), BF16),
                pltpu.SemaphoreType.DMA((TILES,)),
            ],
        ),
        out_shape=jax.ShapeDtypeStruct(state_rows.shape, BF16),
        compiler_params=params(),
        name="new_states",
    )(added_table, state_rows, messages, *fixed, *first)

    mixed = pl.pallas_call(
        norm_kernel,
        grid=(1,),
        in_specs=[whole(tile_shape), whole(all_squares.shape), whole(gain_row.shape)],
        out_specs=whole(tile_shape),
        out_shape=jax.ShapeDtypeStruct(tile_shape, BF16),
        compiler_params=params(),
        name="norm",
    )(gated, all_squares, gain_row)
    return (mixed, new_states.reshape(states.shape))


def solution(mesh):
    in_specs = (
        P("dp", None, "tensor"),
        P("dp", None, "tensor"),
        P("dp", None, None),
        P("dp", None, None),
        P("dp", "tensor", None),
        P("tensor"),
        P("tensor"),
        P("tensor"),
        P("dp", "tensor", None, None),
        P(),
        P(),
    )
    out_specs = (P("dp", None, "tensor"), P("dp", "tensor", None, None))
    return jax.shard_map(
        on_device, mesh=mesh, in_specs=in_specs, out_specs=out_specs, check_vma=False
    )
```

```python
import functools

import jax
import jax.numpy as jnp
from jax import lax
from jax.experimental import pallas as pl
from jax.experimental.pallas import tpu as pltpu
from jax.sharding import PartitionSpec as P

GROUPS = 4
PLACES = 16
TILES = 8
HEADS_DEV = 4
HEAD_DIM = 64
STATE = 256
ROWS = 128
WIDTH = HEADS_DEV * HEAD_DIM
TAIL = 16
MESSAGE = WIDTH + TAIL
NORM_WIDTH = 2048.0
FIXED = ((8, 0), (1, 0), (1, 1))
PAIRS = (2, 3, 4, 5, 6, 7)
MIB = 1024 * 1024
F32 = jnp.float32
BF16 = jnp.bfloat16
HBM = pl.BlockSpec(memory_space=pltpu.HBM)
VMEM = pl.BlockSpec(memory_space=pltpu.VMEM)
NN = (((1,), (0,)), ((), ()))
NT = (((1,), (1,)), ((), ()))
TN = (((0,), (0,)), ((), ()))
TABLES = [pltpu.SMEM((PLACES,), jnp.int32)] * 3
TILE_NUMBERS = pltpu.SMEM((PLACES * TILES,), jnp.int32)
HEAD_NUMBERS = pltpu.SMEM((HEADS_DEV,), F32)


def params(mib):
    return pltpu.CompilerParams(vmem_limit_bytes=mib * MIB)


def lane_ids(shape):
    return lax.broadcasted_iota(jnp.int32, shape, len(shape) - 1)


def route(dest_ref, used, sender, rank):
    me = lax.axis_index("dp")
    for o in range(PLACES):
        used[o] = 0
        sender[o] = 0
    for t in range(TILES):
        used[dest_ref[t]] = 1
        sender[lax.rem(dest_ref[me * TILES + t] - me + PLACES, PLACES)] = t
    count = 0
    for g in range(PLACES):
        o = lax.rem(me - g + PLACES, PLACES)
        rank[o] = count
        count = count + used[o]


def side_offsets(k, turn):
    if isinstance(k, int) and k == 8:
        return 8, 8
    mine = jnp.where(lax.rem(lax.axis_index("dp"), 2) == turn, k, PLACES - k)
    return mine, jnp.where(lax.rem(k, 2) == 0, mine, PLACES - mine)


def doubles(used):
    found = [jnp.int32(0), jnp.int32(0)]
    count = jnp.int32(0)
    for k in PAIRS:
        both = used[k] * used[PLACES - k]
        for n in range(2):
            found[n] = jnp.where((both == 1) & (count == n), k, found[n])
        count = count + both
    return found


def against(o):
    return lax.rem(PLACES - o, PLACES)


def step_rows(dt_ref, a_ref, rows_ref):
    for t in range(TILES):
        rows_ref[pl.ds(t * HEADS_DEV, HEADS_DEV), :] = dt_ref[t]
    raw = rows_ref[...]
    step = jnp.maximum(raw, 0.0) + jnp.log1p(jnp.exp(-jnp.abs(raw)))
    head = lax.rem(lax.broadcasted_iota(jnp.int32, raw.shape, 0), HEADS_DEV)
    a_log = jnp.zeros(raw.shape, F32)
    for h in range(HEADS_DEV):
        a_log = jnp.where(head == h, a_ref[h], a_log)
    total = -jnp.exp(a_log) * step
    lanes = lane_ids(total.shape)
    shift = 1
    while shift < ROWS:
        total = total + jnp.where(lanes >= shift, pltpu.roll(total, shift, 1), 0.0)
        shift *= 2
    return step, total


def spread_heads(columns, t):
    low = lane_ids((ROWS, 2 * HEAD_DIM)) < HEAD_DIM
    halves = []
    for j in range(2):
        at = t * HEADS_DEV + 2 * j
        halves.append(jnp.where(low, columns[:, at : at + 1], columns[:, at + 1 : at + 2]))
    return jnp.concatenate(halves, axis=1)


def group_part(ref):
    size = lax.axis_size("tensor") // GROUPS
    first = lax.div(lax.axis_index("tensor"), size) * STATE
    return ref.at[:, :, pl.ds(pl.multiple_of(first, STATE), STATE)]


def act(copies, sems, start):
    for needed, source, target, sem in copies:
        copy = pltpu.make_async_copy(source, target, sems.at[sem])
        step = copy.start if start else copy.wait
        if needed is None:
            step()
        else:
            pl.when(needed)(step)


def added_kernel(dest_hbm, accepted_hbm, a_hbm, x_hbm, b_hbm, dt_hbm, states_hbm, *rest):
    send, fixed, second = rest[0], rest[1:4], rest[4:8]
    dest_ref, accepted_ref, a_ref, x_ref, b_ref, dt_ref, rows_ref, states_ref = rest[8:16]
    added_ref, used, sender, rank, sems, out_sems = rest[16:]
    moves = (
        (dest_hbm, dest_ref),
        (accepted_hbm, accepted_ref),
        (a_hbm, a_ref),
        (dt_hbm, dt_ref),
        (states_hbm, states_ref),
        (x_hbm, x_ref),
        (group_part(b_hbm), b_ref),
    )
    loads = [pltpu.make_async_copy(*move, sems.at[i]) for i, move in enumerate(moves)]
    for load in loads:
        load.start()
    for load in loads[:4]:
        load.wait()
    route(dest_ref, used, sender, rank)
    me = lax.axis_index("dp")
    part = pl.ds(0, WIDTH)
    early, late = [], []
    for i, (k, turn) in enumerate(FIXED):
        o = side_offsets(k, turn)[0]
        early.append((None, states_ref.at[rank[against(o)]], fixed[i], PLACES + i))
    for n, k in enumerate(doubles(used)):
        for turn in (0, 1):
            o = side_offsets(k, turn)[0]
            prefix = states_ref.at[rank[against(o)]]
            early.append((k > 0, prefix, second[2 * n + turn], PLACES + 3 + 2 * n + turn))
    for to in range(PLACES):
        o = lax.rem(to - me + PLACES, PLACES)
        out, back = used[o] == 1, used[against(o)] == 1
        early.append((back & ~out, states_ref.at[rank[against(o)]], send.at[to, part, :], to))
        late.append((out, added_ref.at[sender[o]], send.at[to], to))
    loads[4].wait()
    act(early, out_sems, True)
    step, total = step_rows(dt_ref, a_ref, rows_ref)
    shape = total.shape
    lanes = lane_ids(shape)
    row_tile = lax.div(lax.broadcasted_iota(jnp.int32, shape, 0), HEADS_DEV)
    accepted = jnp.zeros(shape, jnp.int32)
    for t in range(TILES):
        accepted = jnp.where(row_tile == t, accepted_ref[me * TILES + t], accepted)
    final = jnp.sum(jnp.where(lanes == accepted - 1, total, 0.0), axis=1, keepdims=True)
    kept = lanes < accepted
    scale = jnp.where(kept, jnp.exp(jnp.where(kept, final - total, 0.0)), 0.0) * step
    columns = jnp.transpose(scale)
    fade = jnp.broadcast_to(jnp.exp(final), (shape[0], STATE))
    fade_high = fade.astype(BF16).astype(F32)
    fade_low = fade - fade_high
    empty = jnp.zeros((TAIL - 2 * HEADS_DEV, STATE), F32)
    for load in loads[5:]:
        load.wait()
    for t in range(TILES):
        x_kept = (x_ref[t].astype(F32) * spread_heads(columns, t)).astype(BF16)
        added = lax.dot_general(x_kept, b_ref[t], TN, preferred_element_type=F32)
        added_ref[t, part, :] = added.astype(BF16)
        at = t * HEADS_DEV
        tail = jnp.concatenate(
            [fade_high[at : at + HEADS_DEV], fade_low[at : at + HEADS_DEV], empty], axis=0
        )
        added_ref[t, pl.ds(WIDTH, TAIL), :] = tail.astype(BF16)
    act(late, out_sems, True)
    act(early, out_sems, False)
    act(late, out_sems, False)


def within_kernel(a_hbm, d_hbm, x_hbm, b_hbm, c_hbm, z_hbm, dt_hbm, *rest):
    out_ref, fade_ref, silu_ref, a_ref, d_ref, c_ref, x_ref, b_ref, z_ref, dt_ref = rest[:10]
    rows_ref, sems = rest[10:]
    moves = (
        (a_hbm, a_ref),
        (d_hbm, d_ref),
        (dt_hbm, dt_ref),
        (z_hbm, z_ref),
        (group_part(c_hbm), c_ref),
        (group_part(b_hbm), b_ref),
        (x_hbm, x_ref),
    )
    loads = [pltpu.make_async_copy(*move, sems.at[i]) for i, move in enumerate(moves)]
    for load in loads:
        load.start()
    for load in loads[:3]:
        load.wait()
    step, total = step_rows(dt_ref, a_ref, rows_ref)
    columns = jnp.transpose(total)
    fade_ref[...] = jnp.exp(columns)
    lower = lane_ids((ROWS, ROWS)) <= lax.broadcasted_iota(jnp.int32, (ROWS, ROWS), 0)
    wide = lax.div(lane_ids((ROWS, WIDTH)), HEAD_DIM)
    head = lax.div(lane_ids((1, WIDTH)), HEAD_DIM)
    skip = jnp.zeros((1, WIDTH), F32)
    for h in range(HEADS_DEV):
        skip = jnp.where(head == h, d_ref[h], skip)
    for load in loads[3:]:
        load.wait()
    for t in range(TILES):
        z = z_ref[t].astype(F32)
        silu_ref[t] = z / (1.0 + jnp.exp(-z))
        products = lax.dot_general(c_ref[t], b_ref[t], NT, preferred_element_type=F32)
        x = x_ref[t]
        weights = []
        inputs = []
        for h in range(HEADS_DEV):
            at = t * HEADS_DEV + h
            gap = columns[:, at : at + 1] - total[at : at + 1, :]
            decay = jnp.exp(jnp.where(lower, gap, -1e30))
            weights.append((products * decay * step[at : at + 1, :]).astype(BF16))
            inputs.append(jnp.where(wide == h, x, jnp.zeros_like(x)))
        within = lax.dot_general(
            jnp.concatenate(weights, axis=1),
            jnp.concatenate(inputs, axis=0),
            NN,
            preferred_element_type=F32,
        )
        out_ref[t] = within + skip * x.astype(F32)


def gate_kernel(dest_hbm, c_hbm, silu_hbm, within_hbm, fade_hbm, states_hbm, got, *rest):
    fixed, second = rest[:3], rest[3:7]
    gated_hbm, squares_ref, dest_ref, c_ref, silu_ref, within_ref, fade_ref = rest[7:14]
    held_ref, gated_ref, used, sender, rank, sems, held_sems, out_sems = rest[14:]
    moves = (
        (dest_hbm, dest_ref),
        (fade_hbm, fade_ref),
        (group_part(c_hbm), c_ref),
        (within_hbm, within_ref),
        (silu_hbm, silu_ref),
    )
    loads = [pltpu.make_async_copy(*move, sems.at[i]) for i, move in enumerate(moves)]
    for load in loads:
        load.start()
    loads[0].wait()
    route(dest_ref, used, sender, rank)
    part = pl.ds(0, WIDTH)
    me = lax.axis_index("dp")
    copies = [(used[0] == 1, states_hbm.at[rank[0]], sender[0])]
    for i, (k, turn) in enumerate(FIXED):
        copies.append((None, fixed[i], sender[against(side_offsets(k, turn)[1])]))
    for n, k in enumerate(doubles(used)):
        for turn in (0, 1):
            o = against(side_offsets(k, turn)[1])
            copies.append((k > 0, second[2 * n + turn], sender[o]))
    for origin in range(PLACES):
        o = lax.rem(me - origin + PLACES, PLACES)
        needed = (used[against(o)] == 1) & (used[o] == 0)
        copies.append((needed, got.at[origin, part, :], sender[against(o)]))
    copies = [(needed, source, held_ref.at[t], t) for needed, source, t in copies]
    act(copies, held_sems, True)
    for load in loads[1:]:
        load.wait()
    columns = fade_ref[...]
    lanes = lane_ids((ROWS, ROWS))
    squares = jnp.zeros((ROWS, ROWS), F32)
    outs = []
    for t in range(TILES):
        pltpu.make_async_copy(states_hbm.at[0], held_ref.at[t], held_sems.at[t]).wait()
        carried = lax.dot_general(c_ref[t], held_ref[t], NT, preferred_element_type=F32)
        total = within_ref[t] + spread_heads(columns, t) * carried
        gated = total.astype(BF16).astype(F32) * silu_ref[t]
        gated_ref[t] = gated
        outs.append(pltpu.make_async_copy(gated_ref.at[t], gated_hbm.at[t], out_sems.at[t]))
        outs[-1].start()
        squares = jnp.where(lanes == t, jnp.sum(gated * gated, axis=1, keepdims=True), squares)
    turned = jnp.transpose(squares)[:TILES]
    for i in range(squares_ref.shape[0]):
        squares_ref[i] = turned
    for out in outs:
        out.wait()


def norm_kernel(gated_hbm, squares_ref, gain_ref, out_hbm, gated_ref, out_ref, load_sems, sems):
    loads = []
    for t in range(TILES):
        loads.append(pltpu.make_async_copy(gated_hbm.at[t], gated_ref.at[t], load_sems.at[t]))
        loads[-1].start()
    total = jnp.sum(squares_ref[...], axis=0)
    factor = lax.rsqrt(total / NORM_WIDTH + 1e-05)
    filled = jnp.concatenate([factor, jnp.zeros((ROWS - TILES, ROWS), F32)], axis=0)
    columns = jnp.transpose(filled)
    gain = gain_ref[...]
    copies = []
    for t in range(TILES):
        loads[t].wait()
        out_ref[t] = (gated_ref[t] * columns[:, t : t + 1] * gain).astype(BF16)
        copies.append(pltpu.make_async_copy(out_ref.at[t], out_hbm.at[t], sems.at[t]))
        copies[-1].start()
    for copy in copies:
        copy.wait()


def state_kernel(dest_hbm, states_hbm, got, out_hbm, *rest):
    dest_ref, states_ref, held_ref, out_ref, used, sender, rank, sems, held_sems, out_sems = rest
    loads = [
        pltpu.make_async_copy(dest_hbm, dest_ref, sems.at[0]),
        pltpu.make_async_copy(states_hbm, states_ref, sems.at[1]),
    ]
    for load in loads:
        load.start()
    loads[0].wait()
    route(dest_ref, used, sender, rank)
    me = lax.axis_index("dp")
    copies = []
    for origin in range(PLACES):
        o = lax.rem(me - origin + PLACES, PLACES)
        copies.append((used[o] == 1, got.at[origin], held_ref.at[rank[o]], rank[o]))
    act(copies, held_sems, True)
    loads[1].wait()
    outs = []
    for t in range(TILES):
        pltpu.make_async_copy(got.at[0], held_ref.at[t], held_sems.at[t]).wait()
        tail = held_ref[t, pl.ds(WIDTH, TAIL), :].astype(F32)
        for h in range(HEADS_DEV):
            rows = pl.ds(h * HEAD_DIM, HEAD_DIM)
            fade = tail[h : h + 1] + tail[HEADS_DEV + h : HEADS_DEV + h + 1]
            out_ref[t, rows, :] = (
                fade * states_ref[t, rows, :].astype(F32) + held_ref[t, rows, :].astype(F32)
            ).astype(BF16)
        outs.append(pltpu.make_async_copy(out_ref.at[t], out_hbm.at[t], out_sems.at[t]))
        outs[-1].start()
    for out in outs:
        out.wait()


def shifted(message, k, turn):
    pairs = []
    for g in range(PLACES):
        forth = k if k == 8 or g % 2 == turn else PLACES - k
        pairs.append((g, (g + forth) % PLACES))
    return lax.ppermute(message, "dp", pairs)


def exchange_second(k, second):
    if k == 0:
        return tuple(jnp.zeros((WIDTH, STATE), BF16) for _ in (0, 1))
    return tuple(shifted(second[turn], k, turn) for turn in (0, 1))


def on_device(x_in, z_in, b_in, c_in, dt_raw, a_log, d_skip, norm_gain, states, dest, accepted):
    group_size = lax.axis_size("tensor") // GROUPS
    gain_row = norm_gain.reshape(1, WIDTH)
    state_rows = states.reshape(TILES, WIDTH, STATE)
    tile_shape = (TILES, ROWS, WIDTH)
    prefix = jax.ShapeDtypeStruct((WIDTH, STATE), BF16)
    messages = jax.ShapeDtypeStruct((PLACES, MESSAGE, STATE), BF16)
    state_scratch = pltpu.VMEM(state_rows.shape, BF16)
    message_scratch = pltpu.VMEM((TILES, MESSAGE, STATE), BF16)
    wide_scratch = pltpu.VMEM(tile_shape, F32)
    rows_scratch = pltpu.VMEM((TILES * HEADS_DEV, ROWS), F32)
    tile_scratch = pltpu.VMEM(tile_shape, BF16)
    dt_scratch = pltpu.VMEM(dt_raw.shape, F32)
    dma = pltpu.SemaphoreType.DMA

    pairs = jnp.array(PAIRS, jnp.int32)[:, None]
    hits = jnp.sum((dest[None, :TILES] == pairs) | (dest[None, :TILES] == PLACES - pairs), axis=1)
    both = hits == 2
    order = jnp.arange(len(PAIRS), dtype=jnp.int32)
    earlier = jnp.sum(both[None, :] & (order[None, :] < order[:, None]), axis=1)
    second_codes = [jnp.sum(jnp.where(both & (earlier == n), order + 1, 0)) for n in range(2)]

    sent = pl.pallas_call(
        added_kernel,
        in_specs=[HBM] * 7,
        out_specs=[HBM] * 8,
        out_shape=[messages] + [prefix] * 7,
        scratch_shapes=[
            TILE_NUMBERS,
            TILE_NUMBERS,
            HEAD_NUMBERS,
            tile_scratch,
            tile_scratch,
            dt_scratch,
            rows_scratch,
            state_scratch,
            message_scratch,
            *TABLES,
            dma((7,)),
            dma((PLACES + 7,)),
        ],
        compiler_params=params(54),
        name="added",
    )(dest, accepted, a_log, x_in, b_in, dt_raw, state_rows)
    send, sent_fixed, sent_second = sent[0], sent[1:4], sent[4:8]

    fixed = [shifted(value, k, turn) for value, (k, turn) in zip(sent_fixed, FIXED)]
    got = lax.all_to_all(send, "dp", split_axis=0, concat_axis=0, tiled=True)

    local = pl.pallas_call(
        within_kernel,
        in_specs=[HBM] * 7,
        out_specs=[VMEM] * 3,
        out_shape=[
            jax.ShapeDtypeStruct(tile_shape, F32),
            jax.ShapeDtypeStruct((ROWS, TILES * HEADS_DEV), F32),
            jax.ShapeDtypeStruct(tile_shape, F32),
        ],
        scratch_shapes=[
            HEAD_NUMBERS,
            HEAD_NUMBERS,
            tile_scratch,
            tile_scratch,
            tile_scratch,
            tile_scratch,
            dt_scratch,
            rows_scratch,
            dma((7,)),
        ],
        compiler_params=params(52),
        name="within",
    )(a_log, d_skip, x_in, b_in, c_in, z_in, dt_raw)

    local, sent_second, second_codes = lax.optimization_barrier((local, sent_second, second_codes))
    within, fade, silu = local
    branches = [functools.partial(exchange_second, k) for k in (0,) + PAIRS]
    later = lax.switch(second_codes[1], branches, sent_second[2:])
    second = lax.switch(second_codes[0], branches, sent_second[:2]) + later

    gated, squares = pl.pallas_call(
        gate_kernel,
        in_specs=[HBM] * 14,
        out_specs=[HBM, VMEM],
        out_shape=[
            jax.ShapeDtypeStruct(tile_shape, F32),
            jax.ShapeDtypeStruct((group_size, TILES, ROWS), F32),
        ],
        scratch_shapes=[
            TILE_NUMBERS,
            tile_scratch,
            wide_scratch,
            wide_scratch,
            pltpu.VMEM((ROWS, TILES * HEADS_DEV), F32),
            state_scratch,
            wide_scratch,
            *TABLES,
            dma((5,)),
            dma((TILES,)),
            dma((TILES,)),
        ],
        compiler_params=params(54),
        name="gate",
    )(dest, c_in, silu, within, fade, state_rows, got, *fixed, *second)

    members = [list(range(g * group_size, (g + 1) * group_size)) for g in range(GROUPS)]
    all_squares = lax.all_to_all(
        squares, "tensor", split_axis=0, concat_axis=0, axis_index_groups=members, tiled=True
    )

    new_states = pl.pallas_call(
        state_kernel,
        in_specs=[HBM] * 3,
        out_specs=HBM,
        out_shape=jax.ShapeDtypeStruct(state_rows.shape, BF16),
        scratch_shapes=[
            TILE_NUMBERS,
            state_scratch,
            message_scratch,
            state_scratch,
            *TABLES,
            dma((2,)),
            dma((TILES,)),
            dma((TILES,)),
        ],
        compiler_params=params(54),
        name="new_states",
    )(dest, state_rows, got)

    mixed = pl.pallas_call(
        norm_kernel,
        in_specs=[HBM, VMEM, VMEM],
        out_specs=HBM,
        out_shape=jax.ShapeDtypeStruct(tile_shape, BF16),
        scratch_shapes=[wide_scratch, tile_scratch, dma((TILES,)), dma((TILES,))],
        compiler_params=params(54),
        name="norm",
    )(gated, all_squares, gain_row)
    return (mixed, new_states.reshape(states.shape))


def solution(mesh):
    in_specs = (
        P("dp", None, "tensor"),
        P("dp", None, "tensor"),
        P("dp", None, None),
        P("dp", None, None),
        P("dp", "tensor", None),
        P("tensor"),
        P("tensor"),
        P("tensor"),
        P("dp", "tensor", None, None),
        P(),
        P(),
    )
    out_specs = (P("dp", None, "tensor"), P("dp", "tensor", None, None))
    return jax.shard_map(
        on_device, mesh=mesh, in_specs=in_specs, out_specs=out_specs, check_vma=False
    )
```

```python
import functools

import jax
import jax.numpy as jnp
from jax import lax
from jax.experimental import pallas as pl
from jax.experimental.pallas import tpu as pltpu
from jax.sharding import PartitionSpec as P

GROUPS = 4
PLACES = 16
TILES = 8
HEADS_DEV = 4
HEAD_DIM = 64
STATE = 256
ROWS = 128
WIDTH = HEADS_DEV * HEAD_DIM
TAIL = 16
MESSAGE = WIDTH + TAIL
NORM_WIDTH = 2048.0
FIXED = ((8, 0), (1, 0), (1, 1))
PAIRS = (2, 3, 4, 5, 6, 7)
VMEM_BYTES = 63471616
F32 = jnp.float32
BF16 = jnp.bfloat16
ANY = pl.BlockSpec(memory_space=pl.ANY)
HBM = pl.BlockSpec(memory_space=pltpu.HBM)
VMEM = pl.BlockSpec(memory_space=pltpu.VMEM)
NN = (((1,), (0,)), ((), ()))
NT = (((1,), (1,)), ((), ()))
TN = (((0,), (0,)), ((), ()))
TABLES = [pltpu.SMEM((PLACES,), jnp.int32)] * 3
TILE_NUMBERS = pltpu.SMEM((PLACES * TILES,), jnp.int32)
HEAD_NUMBERS = pltpu.SMEM((HEADS_DEV,), F32)


def params(room=0):
    return pltpu.CompilerParams(vmem_limit_bytes=VMEM_BYTES - room)


def lane_ids(shape):
    return lax.broadcasted_iota(jnp.int32, shape, len(shape) - 1)


def route(dest_ref, used, sender, rank):
    me = lax.axis_index("dp")
    for o in range(PLACES):
        used[o] = 0
        sender[o] = 0
    for t in range(TILES):
        used[dest_ref[t]] = 1
        sender[lax.rem(dest_ref[me * TILES + t] - me + PLACES, PLACES)] = t
    count = 0
    for g in range(PLACES):
        o = lax.rem(me - g + PLACES, PLACES)
        rank[o] = count
        count = count + used[o]


def side_offsets(k, turn):
    if isinstance(k, int) and k == 8:
        return 8, 8
    mine = jnp.where(lax.rem(lax.axis_index("dp"), 2) == turn, k, PLACES - k)
    return mine, jnp.where(lax.rem(k, 2) == 0, mine, PLACES - mine)


def doubles(used):
    found = [jnp.int32(0), jnp.int32(0)]
    count = jnp.int32(0)
    for k in PAIRS:
        both = used[k] * used[PLACES - k]
        for n in range(2):
            found[n] = jnp.where((both == 1) & (count == n), k, found[n])
        count = count + both
    return found


def against(o):
    return lax.rem(PLACES - o, PLACES)


def step_rows(dt_ref, a_ref, rows_ref):
    for t in range(TILES):
        rows_ref[pl.ds(t * HEADS_DEV, HEADS_DEV), :] = dt_ref[t]
    raw = rows_ref[...]
    step = jnp.maximum(raw, 0.0) + jnp.log1p(jnp.exp(-jnp.abs(raw)))
    head = lax.rem(lax.broadcasted_iota(jnp.int32, raw.shape, 0), HEADS_DEV)
    a_log = jnp.zeros(raw.shape, F32)
    for h in range(HEADS_DEV):
        a_log = jnp.where(head == h, a_ref[h], a_log)
    total = -jnp.exp(a_log) * step
    lanes = lane_ids(total.shape)
    shift = 1
    while shift < ROWS:
        total = total + jnp.where(lanes >= shift, pltpu.roll(total, shift, 1), 0.0)
        shift *= 2
    return step, total


def spread_heads(columns, t):
    low = lane_ids((ROWS, 2 * HEAD_DIM)) < HEAD_DIM
    halves = []
    for j in range(2):
        at = t * HEADS_DEV + 2 * j
        halves.append(jnp.where(low, columns[:, at : at + 1], columns[:, at + 1 : at + 2]))
    return jnp.concatenate(halves, axis=1)


def group_part(ref):
    size = lax.axis_size("tensor") // GROUPS
    first = lax.div(lax.axis_index("tensor"), size) * STATE
    return ref.at[:, :, pl.ds(pl.multiple_of(first, STATE), STATE)]


def act(copies, sems, start):
    for needed, source, target, sem in copies:
        copy = pltpu.make_async_copy(source, target, sems.at[sem])
        step = copy.start if start else copy.wait
        if needed is None:
            step()
        else:
            pl.when(needed)(step)


def added_kernel(dest_hbm, accepted_hbm, a_hbm, x_hbm, b_hbm, dt_hbm, states_hbm, *rest):
    send, fixed, second = rest[0], rest[1:4], rest[4:8]
    dest_ref, accepted_ref, a_ref, x_ref, b_ref, dt_ref, rows_ref, states_ref = rest[8:16]
    added_ref, used, sender, rank, sems, out_sems = rest[16:]
    moves = (
        (dest_hbm, dest_ref),
        (accepted_hbm, accepted_ref),
        (a_hbm, a_ref),
        (dt_hbm, dt_ref),
        (states_hbm, states_ref),
        (x_hbm, x_ref),
        (group_part(b_hbm), b_ref),
    )
    loads = [pltpu.make_async_copy(*move, sems.at[i]) for i, move in enumerate(moves)]
    for load in loads:
        load.start()
    for load in loads[:4]:
        load.wait()
    route(dest_ref, used, sender, rank)
    me = lax.axis_index("dp")
    part = pl.ds(0, WIDTH)
    early = []
    for to in range(PLACES):
        o = lax.rem(to - me + PLACES, PLACES)
        needed = (used[against(o)] == 1) & (o != 0)
        early.append((needed, states_ref.at[rank[against(o)]], send.at[to, part, :], to))
    step, total = step_rows(dt_ref, a_ref, rows_ref)
    shape = total.shape
    lanes = lane_ids(shape)
    row_tile = lax.div(lax.broadcasted_iota(jnp.int32, shape, 0), HEADS_DEV)
    accepted = jnp.zeros(shape, jnp.int32)
    for t in range(TILES):
        accepted = jnp.where(row_tile == t, accepted_ref[me * TILES + t], accepted)
    final = jnp.sum(jnp.where(lanes == accepted - 1, total, 0.0), axis=1, keepdims=True)
    kept = lanes < accepted
    scale = jnp.where(kept, jnp.exp(jnp.where(kept, final - total, 0.0)), 0.0) * step
    columns = jnp.transpose(scale)
    fade = jnp.broadcast_to(jnp.exp(final), (shape[0], STATE))
    fade_high = fade.astype(BF16).astype(F32)
    fade_low = fade - fade_high
    empty = jnp.zeros((TAIL - 2 * HEADS_DEV, STATE), F32)
    loads[4].wait()
    act(early, out_sems, True)
    for load in loads[5:]:
        load.wait()
    late = []
    for t in range(TILES):
        x_kept = (x_ref[t].astype(F32) * spread_heads(columns, t)).astype(BF16)
        added = lax.dot_general(x_kept, b_ref[t], TN, preferred_element_type=F32)
        added_ref[t, part, :] = added.astype(BF16)
        at = t * HEADS_DEV
        tail = jnp.concatenate(
            [fade_high[at : at + HEADS_DEV], fade_low[at : at + HEADS_DEV], empty], axis=0
        )
        added_ref[t, pl.ds(WIDTH, TAIL), :] = tail.astype(BF16)
        to = dest_ref[me * TILES + t]
        o = lax.rem(to - me + PLACES, PLACES)
        late.append(((used[against(o)] == 0) | (o == 0), added_ref.at[t], send.at[to], to))
        act(late[-1:], out_sems, True)
    seconds = []
    for i, (k, turn) in enumerate(FIXED):
        o = side_offsets(k, turn)[0]
        seconds.append((None, added_ref.at[sender[o]], fixed[i], PLACES + i))
    for n, k in enumerate(doubles(used)):
        for turn in (0, 1):
            o = side_offsets(k, turn)[0]
            i = 2 * n + turn
            seconds.append((k > 0, added_ref.at[sender[o]], second[i], PLACES + 3 + i))
    act(seconds, out_sems, True)
    late += seconds
    act(early, out_sems, False)
    act(late, out_sems, False)


def within_kernel(a_hbm, d_hbm, x_hbm, b_hbm, c_hbm, z_hbm, dt_hbm, *rest):
    out_ref, fade_ref, silu_ref, a_ref, d_ref, c_ref, x_ref, b_ref, z_ref, dt_ref = rest[:10]
    rows_ref, sems = rest[10:]
    moves = (
        (a_hbm, a_ref),
        (d_hbm, d_ref),
        (dt_hbm, dt_ref),
        (z_hbm, z_ref),
        (group_part(c_hbm), c_ref),
        (group_part(b_hbm), b_ref),
        (x_hbm, x_ref),
    )
    loads = [pltpu.make_async_copy(*move, sems.at[i]) for i, move in enumerate(moves)]
    for load in loads:
        load.start()
    for load in loads[:3]:
        load.wait()
    step, total = step_rows(dt_ref, a_ref, rows_ref)
    columns = jnp.transpose(total)
    fade_ref[...] = jnp.exp(columns)
    lower = lane_ids((ROWS, ROWS)) <= lax.broadcasted_iota(jnp.int32, (ROWS, ROWS), 0)
    wide = lax.div(lane_ids((ROWS, WIDTH)), HEAD_DIM)
    head = lax.div(lane_ids((1, WIDTH)), HEAD_DIM)
    skip = jnp.zeros((1, WIDTH), F32)
    for h in range(HEADS_DEV):
        skip = jnp.where(head == h, d_ref[h], skip)
    for load in loads[3:]:
        load.wait()
    for t in range(TILES):
        z = z_ref[t].astype(F32)
        silu_ref[t] = z / (1.0 + jnp.exp(-z))
        products = lax.dot_general(c_ref[t], b_ref[t], NT, preferred_element_type=F32)
        x = x_ref[t]
        weights = []
        inputs = []
        for h in range(HEADS_DEV):
            at = t * HEADS_DEV + h
            gap = columns[:, at : at + 1] - total[at : at + 1, :]
            decay = jnp.exp(jnp.where(lower, gap, -1e30))
            weights.append((products * decay * step[at : at + 1, :]).astype(BF16))
            inputs.append(jnp.where(wide == h, x, jnp.zeros_like(x)))
        within = lax.dot_general(
            jnp.concatenate(weights, axis=1),
            jnp.concatenate(inputs, axis=0),
            NN,
            preferred_element_type=F32,
        )
        out_ref[t] = within + skip * x.astype(F32)


def gate_kernel(dest_hbm, c_hbm, silu_hbm, within_hbm, fade_hbm, states_hbm, got, *rest):
    gated_hbm, squares_hbm = rest[:2]
    dest_ref, c_ref, silu_ref, within_ref, fade_ref, held_ref, gated_ref = rest[2:9]
    squares_ref, used, sender, rank, sems, held_sems, out_sems = rest[9:]
    moves = (
        (dest_hbm, dest_ref),
        (fade_hbm, fade_ref),
        (group_part(c_hbm), c_ref),
        (within_hbm, within_ref),
        (silu_hbm, silu_ref),
    )
    loads = [pltpu.make_async_copy(*move, sems.at[i]) for i, move in enumerate(moves)]
    for load in loads:
        load.start()
    loads[0].wait()
    route(dest_ref, used, sender, rank)
    part = pl.ds(0, WIDTH)
    me = lax.axis_index("dp")
    copies = [(used[0] == 1, states_hbm.at[rank[0]], sender[0])]
    for origin in range(PLACES):
        o = lax.rem(me - origin + PLACES, PLACES)
        needed = (used[against(o)] == 1) & (o != 0)
        copies.append((needed, got.at[origin, part, :], sender[against(o)]))
    copies = [(needed, source, held_ref.at[t], t) for needed, source, t in copies]
    act(copies, held_sems, True)
    for load in loads[1:]:
        load.wait()
    for t in range(TILES):
        pltpu.make_async_copy(states_hbm.at[0], held_ref.at[t], held_sems.at[t]).wait()
    columns = fade_ref[...]
    lanes = lane_ids((ROWS, ROWS))
    squares = jnp.zeros((ROWS, ROWS), F32)
    for t in range(TILES):
        carried = lax.dot_general(c_ref[t], held_ref[t], NT, preferred_element_type=F32)
        total = within_ref[t] + spread_heads(columns, t) * carried
        gated = total.astype(BF16).astype(F32) * silu_ref[t]
        gated_ref[t] = gated
        squares = jnp.where(lanes == t, jnp.sum(gated * gated, axis=1, keepdims=True), squares)
    turned = jnp.transpose(squares)[:TILES]
    for i in range(squares_ref.shape[0]):
        squares_ref[i] = turned
    outs = [
        pltpu.make_async_copy(squares_ref, squares_hbm, out_sems.at[0]),
        pltpu.make_async_copy(gated_ref, gated_hbm, out_sems.at[1]),
    ]
    for out in outs:
        out.start()
    for out in outs:
        out.wait()


def norm_kernel(gated_hbm, squares_hbm, gain_hbm, out_hbm, *rest):
    gated_ref, squares_ref, gain_ref, out_ref, load_sems, sems = rest
    half = TILES // 2
    moves = [(squares_hbm, squares_ref), (gain_hbm, gain_ref)]
    for j in range(2):
        part = pl.ds(j * half, half)
        moves.append((gated_hbm.at[part], gated_ref.at[part]))
    loads = [pltpu.make_async_copy(*move, load_sems.at[i]) for i, move in enumerate(moves)]
    for load in loads:
        load.start()
    for load in loads[:2]:
        load.wait()
    total = jnp.sum(squares_ref[...], axis=0)
    factor = lax.rsqrt(total / NORM_WIDTH + 1e-05)
    filled = jnp.concatenate([factor, jnp.zeros((ROWS - TILES, ROWS), F32)], axis=0)
    columns = jnp.transpose(filled)
    gain = gain_ref[...]
    copies = []
    for j in range(2):
        loads[2 + j].wait()
        for t in range(j * half, (j + 1) * half):
            out_ref[t] = (gated_ref[t] * columns[:, t : t + 1] * gain).astype(BF16)
        part = pl.ds(j * half, half)
        copies.append(pltpu.make_async_copy(out_ref.at[part], out_hbm.at[part], sems.at[j]))
        copies[-1].start()
    for copy in copies:
        copy.wait()


def state_kernel(dest_hbm, states_hbm, got, *rest):
    fixed, second, out_hbm, rest = rest[:3], rest[3:7], rest[7], rest[8:]
    dest_ref, states_ref, held_ref, out_ref, used, sender, rank, sems, held_sems, out_sems = rest
    loads = [
        pltpu.make_async_copy(dest_hbm, dest_ref, sems.at[0]),
        pltpu.make_async_copy(states_hbm, states_ref, sems.at[1]),
    ]
    for load in loads:
        load.start()
    loads[0].wait()
    route(dest_ref, used, sender, rank)
    me = lax.axis_index("dp")
    copies = []
    for i, (k, turn) in enumerate(FIXED):
        slot = rank[side_offsets(k, turn)[1]]
        copies.append((None, fixed[i], held_ref.at[slot], slot))
    for n, k in enumerate(doubles(used)):
        for turn in (0, 1):
            slot = rank[side_offsets(k, turn)[1]]
            copies.append((k > 0, second[2 * n + turn], held_ref.at[slot], slot))
    for origin in range(PLACES):
        o = lax.rem(me - origin + PLACES, PLACES)
        needed = (used[o] == 1) & ((used[against(o)] == 0) | (o == 0))
        copies.append((needed, got.at[origin], held_ref.at[rank[o]], rank[o]))
    act(copies, held_sems, True)
    loads[1].wait()
    outs = []
    for t in range(TILES):
        pltpu.make_async_copy(got.at[0], held_ref.at[t], held_sems.at[t]).wait()
        tail = held_ref[t, pl.ds(WIDTH, TAIL), :].astype(F32)
        for h in range(HEADS_DEV):
            rows = pl.ds(h * HEAD_DIM, HEAD_DIM)
            fade = tail[h : h + 1] + tail[HEADS_DEV + h : HEADS_DEV + h + 1]
            out_ref[t, rows, :] = (
                fade * states_ref[t, rows, :].astype(F32) + held_ref[t, rows, :].astype(F32)
            ).astype(BF16)
        outs.append(pltpu.make_async_copy(out_ref.at[t], out_hbm.at[t], out_sems.at[t]))
        outs[-1].start()
    for out in outs:
        out.wait()


def shifted(message, k, turn):
    pairs = []
    for g in range(PLACES):
        forth = k if k == 8 or g % 2 == turn else PLACES - k
        pairs.append((g, (g + forth) % PLACES))
    return lax.ppermute(message, "dp", pairs)


def exchange_second(k, second):
    if k == 0:
        return tuple(jnp.zeros((MESSAGE, STATE), BF16) for _ in (0, 1))
    return tuple(shifted(second[turn], k, turn) for turn in (0, 1))


def on_device(x_in, z_in, b_in, c_in, dt_raw, a_log, d_skip, norm_gain, states, dest, accepted):
    group_size = lax.axis_size("tensor") // GROUPS
    gain_row = norm_gain.reshape(1, WIDTH)
    state_rows = states.reshape(TILES, WIDTH, STATE)
    tile_shape = (TILES, ROWS, WIDTH)
    message = jax.ShapeDtypeStruct((MESSAGE, STATE), BF16)
    messages = jax.ShapeDtypeStruct((PLACES, MESSAGE, STATE), BF16)
    state_scratch = pltpu.VMEM(state_rows.shape, BF16)
    message_scratch = pltpu.VMEM((TILES, MESSAGE, STATE), BF16)
    wide_scratch = pltpu.VMEM(tile_shape, F32)
    rows_scratch = pltpu.VMEM((TILES * HEADS_DEV, ROWS), F32)
    tile_scratch = pltpu.VMEM(tile_shape, BF16)
    dt_scratch = pltpu.VMEM(dt_raw.shape, F32)
    dma = pltpu.SemaphoreType.DMA

    pairs = jnp.array(PAIRS, jnp.int32)[:, None]
    hits = jnp.sum((dest[None, :TILES] == pairs) | (dest[None, :TILES] == PLACES - pairs), axis=1)
    both = hits == 2
    order = jnp.arange(len(PAIRS), dtype=jnp.int32)
    earlier = jnp.sum(both[None, :] & (order[None, :] < order[:, None]), axis=1)
    second_codes = [jnp.sum(jnp.where(both & (earlier == n), order + 1, 0)) for n in range(2)]

    sent = pl.pallas_call(
        added_kernel,
        in_specs=[HBM] * 7,
        out_specs=[HBM] * 8,
        out_shape=[messages] + [message] * 7,
        scratch_shapes=[
            TILE_NUMBERS,
            TILE_NUMBERS,
            HEAD_NUMBERS,
            tile_scratch,
            tile_scratch,
            dt_scratch,
            rows_scratch,
            state_scratch,
            message_scratch,
            *TABLES,
            dma((7,)),
            dma((PLACES + 7,)),
        ],
        compiler_params=params(),
        name="added",
    )(dest, accepted, a_log, x_in, b_in, dt_raw, state_rows)
    send, sent_fixed, sent_second = sent[0], sent[1:4], sent[4:8]

    fixed = [shifted(value, k, turn) for value, (k, turn) in zip(sent_fixed, FIXED)]
    got = lax.all_to_all(send, "dp", split_axis=0, concat_axis=0, tiled=True)

    local = pl.pallas_call(
        within_kernel,
        in_specs=[HBM] * 7,
        out_specs=[VMEM] * 3,
        out_shape=[
            jax.ShapeDtypeStruct(tile_shape, F32),
            jax.ShapeDtypeStruct((ROWS, TILES * HEADS_DEV), F32),
            jax.ShapeDtypeStruct(tile_shape, F32),
        ],
        scratch_shapes=[
            HEAD_NUMBERS,
            HEAD_NUMBERS,
            tile_scratch,
            tile_scratch,
            tile_scratch,
            tile_scratch,
            dt_scratch,
            rows_scratch,
            dma((7,)),
        ],
        compiler_params=params(),
        name="within",
    )(a_log, d_skip, x_in, b_in, c_in, z_in, dt_raw)

    local, sent_second, second_codes = lax.optimization_barrier((local, sent_second, second_codes))
    within, fade, silu = local
    branches = [functools.partial(exchange_second, k) for k in (0,) + PAIRS]
    later = lax.switch(second_codes[1], branches, sent_second[2:])
    later, sent_second = lax.optimization_barrier((later, sent_second))
    second = lax.switch(second_codes[0], branches, sent_second[:2]) + later
    within, second = lax.optimization_barrier((within, second))

    gated, squares = pl.pallas_call(
        gate_kernel,
        in_specs=[HBM] * 6 + [ANY],
        out_specs=[HBM] * 2,
        out_shape=[
            jax.ShapeDtypeStruct(tile_shape, F32),
            jax.ShapeDtypeStruct((group_size, TILES, ROWS), F32),
        ],
        scratch_shapes=[
            TILE_NUMBERS,
            tile_scratch,
            wide_scratch,
            wide_scratch,
            pltpu.VMEM((ROWS, TILES * HEADS_DEV), F32),
            state_scratch,
            wide_scratch,
            pltpu.VMEM((group_size, TILES, ROWS), F32),
            *TABLES,
            dma((5,)),
            dma((TILES,)),
            dma((2,)),
        ],
        compiler_params=params(4500000),
        name="gate",
    )(dest, c_in, silu, within, fade, state_rows, got)

    members = [list(range(g * group_size, (g + 1) * group_size)) for g in range(GROUPS)]
    all_squares = lax.all_to_all(
        squares, "tensor", split_axis=0, concat_axis=0, axis_index_groups=members, tiled=True
    )

    new_states = pl.pallas_call(
        state_kernel,
        in_specs=[HBM] * 2 + [ANY] * 8,
        out_specs=HBM,
        out_shape=jax.ShapeDtypeStruct(state_rows.shape, BF16),
        scratch_shapes=[
            TILE_NUMBERS,
            state_scratch,
            message_scratch,
            state_scratch,
            *TABLES,
            dma((2,)),
            dma((TILES,)),
            dma((TILES,)),
        ],
        compiler_params=params(4500000),
        name="new_states",
    )(dest, state_rows, got, *fixed, *second)

    mixed = pl.pallas_call(
        norm_kernel,
        in_specs=[HBM, ANY, HBM],
        out_specs=HBM,
        out_shape=jax.ShapeDtypeStruct(tile_shape, BF16),
        scratch_shapes=[
            wide_scratch,
            pltpu.VMEM((group_size, TILES, ROWS), F32),
            pltpu.VMEM((1, WIDTH), F32),
            tile_scratch,
            dma((4,)),
            dma((2,)),
        ],
        compiler_params=params(400000),
        name="norm",
    )(gated, all_squares, gain_row)
    return (mixed, new_states.reshape(states.shape))


def solution(mesh):
    in_specs = (
        P("dp", None, "tensor"),
        P("dp", None, "tensor"),
        P("dp", None, None),
        P("dp", None, None),
        P("dp", "tensor", None),
        P("tensor"),
        P("tensor"),
        P("tensor"),
        P("dp", "tensor", None, None),
        P(),
        P(),
    )
    out_specs = (P("dp", None, "tensor"), P("dp", "tensor", None, None))
    return jax.shard_map(
        on_device, mesh=mesh, in_specs=in_specs, out_specs=out_specs, check_vma=False
    )
```

```python
import functools

import jax
import jax.numpy as jnp
from jax import lax
from jax.experimental import pallas as pl
from jax.experimental.pallas import tpu as pltpu
from jax.sharding import PartitionSpec as P

GROUPS = 4
PLACES = 16
TILES = 8
HEADS_DEV = 4
HEAD_DIM = 64
STATE = 256
ROWS = 128
WIDTH = HEADS_DEV * HEAD_DIM
TAIL = 16
MESSAGE = WIDTH + TAIL
NORM_WIDTH = 2048.0
FIXED = ((8, 0), (1, 0), (1, 1))
PAIRS = (2, 3, 4, 5, 6, 7)
VMEM_BYTES = 63471616
F32 = jnp.float32
BF16 = jnp.bfloat16
ANY = pl.BlockSpec(memory_space=pl.ANY)
HBM = pl.BlockSpec(memory_space=pltpu.HBM)
VMEM = pl.BlockSpec(memory_space=pltpu.VMEM)
NN = (((1,), (0,)), ((), ()))
NT = (((1,), (1,)), ((), ()))
TN = (((0,), (0,)), ((), ()))
TABLES = [pltpu.SMEM((PLACES,), jnp.int32)] * 3
TILE_NUMBERS = pltpu.SMEM((PLACES * TILES,), jnp.int32)
HEAD_NUMBERS = pltpu.SMEM((HEADS_DEV,), F32)


def params(room=0):
    return pltpu.CompilerParams(vmem_limit_bytes=VMEM_BYTES - room)


def lane_ids(shape):
    return lax.broadcasted_iota(jnp.int32, shape, len(shape) - 1)


def route(dest_ref, used, sender, rank):
    me = lax.axis_index("dp")
    for o in range(PLACES):
        used[o] = 0
        sender[o] = 0
    for t in range(TILES):
        used[dest_ref[t]] = 1
        sender[lax.rem(dest_ref[me * TILES + t] - me + PLACES, PLACES)] = t
    count = 0
    for g in range(PLACES):
        o = lax.rem(me - g + PLACES, PLACES)
        rank[o] = count
        count = count + used[o]


def side_offsets(k, turn):
    if isinstance(k, int) and k == 8:
        return 8, 8
    mine = jnp.where(lax.rem(lax.axis_index("dp"), 2) == turn, k, PLACES - k)
    return mine, jnp.where(lax.rem(k, 2) == 0, mine, PLACES - mine)


def doubles(used):
    found = [jnp.int32(0), jnp.int32(0)]
    count = jnp.int32(0)
    for k in PAIRS:
        both = used[k] * used[PLACES - k]
        for n in range(2):
            found[n] = jnp.where((both == 1) & (count == n), k, found[n])
        count = count + both
    return found


def against(o):
    return lax.rem(PLACES - o, PLACES)


def step_rows(dt_ref, a_ref, rows_ref):
    for t in range(TILES):
        rows_ref[pl.ds(t * HEADS_DEV, HEADS_DEV), :] = dt_ref[t]
    raw = rows_ref[...]
    step = jnp.maximum(raw, 0.0) + jnp.log1p(jnp.exp(-jnp.abs(raw)))
    head = lax.rem(lax.broadcasted_iota(jnp.int32, raw.shape, 0), HEADS_DEV)
    a_log = jnp.zeros(raw.shape, F32)
    for h in range(HEADS_DEV):
        a_log = jnp.where(head == h, a_ref[h], a_log)
    total = -jnp.exp(a_log) * step
    lanes = lane_ids(total.shape)
    shift = 1
    while shift < ROWS:
        total = total + jnp.where(lanes >= shift, pltpu.roll(total, shift, 1), 0.0)
        shift *= 2
    return step, total


def spread_heads(columns, t):
    low = lane_ids((ROWS, 2 * HEAD_DIM)) < HEAD_DIM
    halves = []
    for j in range(2):
        at = t * HEADS_DEV + 2 * j
        halves.append(jnp.where(low, columns[:, at : at + 1], columns[:, at + 1 : at + 2]))
    return jnp.concatenate(halves, axis=1)


def group_part(ref):
    size = lax.axis_size("tensor") // GROUPS
    first = lax.div(lax.axis_index("tensor"), size) * STATE
    return ref.at[:, :, pl.ds(pl.multiple_of(first, STATE), STATE)]


def act(copies, sems, start):
    for needed, source, target, sem in copies:
        copy = pltpu.make_async_copy(source, target, sems.at[sem])
        step = copy.start if start else copy.wait
        if needed is None:
            step()
        else:
            pl.when(needed)(step)


def added_kernel(dest_hbm, accepted_hbm, a_hbm, x_hbm, b_hbm, dt_hbm, states_hbm, *rest):
    send, fixed, second, codes = rest[0], rest[1:4], rest[4:8], rest[8:10]
    dest_ref, accepted_ref, a_ref, x_ref, b_ref, dt_ref, rows_ref, states_ref = rest[10:18]
    added_ref, used, sender, rank, sems, out_sems = rest[18:]
    moves = (
        (dest_hbm, dest_ref),
        (accepted_hbm, accepted_ref),
        (a_hbm, a_ref),
        (dt_hbm, dt_ref),
        (states_hbm, states_ref),
        (x_hbm, x_ref),
        (group_part(b_hbm), b_ref),
    )
    loads = [pltpu.make_async_copy(*move, sems.at[i]) for i, move in enumerate(moves)]
    for load in loads:
        load.start()
    for load in loads[:4]:
        load.wait()
    route(dest_ref, used, sender, rank)
    me = lax.axis_index("dp")
    part = pl.ds(0, WIDTH)
    early = []
    for to in range(PLACES):
        o = lax.rem(to - me + PLACES, PLACES)
        needed = (used[against(o)] == 1) & (o != 0)
        early.append((needed, states_ref.at[rank[against(o)]], send.at[to, part, :], to))
    step, total = step_rows(dt_ref, a_ref, rows_ref)
    shape = total.shape
    lanes = lane_ids(shape)
    row_tile = lax.div(lax.broadcasted_iota(jnp.int32, shape, 0), HEADS_DEV)
    accepted = jnp.zeros(shape, jnp.int32)
    for t in range(TILES):
        accepted = jnp.where(row_tile == t, accepted_ref[me * TILES + t], accepted)
    final = jnp.sum(jnp.where(lanes == accepted - 1, total, 0.0), axis=1, keepdims=True)
    kept = lanes < accepted
    scale = jnp.where(kept, jnp.exp(jnp.where(kept, final - total, 0.0)), 0.0) * step
    columns = jnp.transpose(scale)
    fade = jnp.broadcast_to(jnp.exp(final), (shape[0], STATE))
    fade_high = fade.astype(BF16).astype(F32)
    fade_low = fade - fade_high
    empty = jnp.zeros((TAIL - 2 * HEADS_DEV, STATE), F32)
    loads[4].wait()
    act(early, out_sems, True)
    for load in loads[5:]:
        load.wait()
    late = []
    for t in range(TILES):
        x_kept = (x_ref[t].astype(F32) * spread_heads(columns, t)).astype(BF16)
        added = lax.dot_general(x_kept, b_ref[t], TN, preferred_element_type=F32)
        added_ref[t, part, :] = added.astype(BF16)
        at = t * HEADS_DEV
        tail = jnp.concatenate(
            [fade_high[at : at + HEADS_DEV], fade_low[at : at + HEADS_DEV], empty], axis=0
        )
        added_ref[t, pl.ds(WIDTH, TAIL), :] = tail.astype(BF16)
        to = dest_ref[me * TILES + t]
        o = lax.rem(to - me + PLACES, PLACES)
        late.append(((used[against(o)] == 0) | (o == 0), added_ref.at[t], send.at[to], to))
        act(late[-1:], out_sems, True)
    seconds = []
    for i, (k, turn) in enumerate(FIXED):
        o = side_offsets(k, turn)[0]
        seconds.append((None, added_ref.at[sender[o]], fixed[i], PLACES + i))
    for n, k in enumerate(doubles(used)):
        codes[n][0] = jnp.maximum(k - 1, 0)
        for turn in (0, 1):
            o = side_offsets(k, turn)[0]
            i = 2 * n + turn
            seconds.append((k > 0, added_ref.at[sender[o]], second[i], PLACES + 3 + i))
    act(seconds, out_sems, True)
    late += seconds
    act(early, out_sems, False)
    act(late, out_sems, False)


def within_kernel(a_hbm, d_hbm, x_hbm, b_hbm, c_hbm, z_hbm, dt_hbm, *rest):
    out_ref, fade_ref, silu_ref, a_ref, d_ref, c_ref, x_ref, b_ref, z_ref, dt_ref = rest[:10]
    rows_ref, sems = rest[10:]
    moves = (
        (a_hbm, a_ref),
        (d_hbm, d_ref),
        (dt_hbm, dt_ref),
        (z_hbm, z_ref),
        (group_part(c_hbm), c_ref),
        (group_part(b_hbm), b_ref),
        (x_hbm, x_ref),
    )
    loads = [pltpu.make_async_copy(*move, sems.at[i]) for i, move in enumerate(moves)]
    for load in loads:
        load.start()
    for load in loads[:3]:
        load.wait()
    step, total = step_rows(dt_ref, a_ref, rows_ref)
    columns = jnp.transpose(total)
    fade_ref[...] = jnp.exp(columns)
    lower = lane_ids((ROWS, ROWS)) <= lax.broadcasted_iota(jnp.int32, (ROWS, ROWS), 0)
    wide = lax.div(lane_ids((ROWS, WIDTH)), HEAD_DIM)
    head = lax.div(lane_ids((1, WIDTH)), HEAD_DIM)
    skip = jnp.zeros((1, WIDTH), F32)
    for h in range(HEADS_DEV):
        skip = jnp.where(head == h, d_ref[h], skip)
    for load in loads[3:]:
        load.wait()
    for t in range(TILES):
        z = z_ref[t].astype(F32)
        silu_ref[t] = z / (1.0 + jnp.exp(-z))
        products = lax.dot_general(c_ref[t], b_ref[t], NT, preferred_element_type=F32)
        x = x_ref[t]
        weights = []
        inputs = []
        for h in range(HEADS_DEV):
            at = t * HEADS_DEV + h
            gap = columns[:, at : at + 1] - total[at : at + 1, :]
            decay = jnp.exp(jnp.where(lower, gap, -1e30))
            weights.append((products * decay * step[at : at + 1, :]).astype(BF16))
            inputs.append(jnp.where(wide == h, x, jnp.zeros_like(x)))
        within = lax.dot_general(
            jnp.concatenate(weights, axis=1),
            jnp.concatenate(inputs, axis=0),
            NN,
            preferred_element_type=F32,
        )
        out_ref[t] = within + skip * x.astype(F32)


def gate_kernel(dest_hbm, c_hbm, silu_hbm, within_hbm, fade_hbm, states_hbm, got, *rest):
    gated_hbm, squares_hbm = rest[:2]
    dest_ref, c_ref, silu_ref, within_ref, fade_ref, held_ref, gated_ref = rest[2:9]
    squares_ref, used, sender, rank, sems, held_sems, out_sems = rest[9:]
    moves = (
        (dest_hbm, dest_ref),
        (fade_hbm, fade_ref),
        (group_part(c_hbm), c_ref),
        (within_hbm, within_ref),
        (silu_hbm, silu_ref),
    )
    loads = [pltpu.make_async_copy(*move, sems.at[i]) for i, move in enumerate(moves)]
    for load in loads:
        load.start()
    loads[0].wait()
    route(dest_ref, used, sender, rank)
    part = pl.ds(0, WIDTH)
    me = lax.axis_index("dp")
    copies = [(used[0] == 1, states_hbm.at[rank[0]], sender[0])]
    for origin in range(PLACES):
        o = lax.rem(me - origin + PLACES, PLACES)
        needed = (used[against(o)] == 1) & (o != 0)
        copies.append((needed, got.at[origin, part, :], sender[against(o)]))
    copies = [(needed, source, held_ref.at[t], t) for needed, source, t in copies]
    act(copies, held_sems, True)
    for load in loads[1:]:
        load.wait()
    for t in range(TILES):
        pltpu.make_async_copy(states_hbm.at[0], held_ref.at[t], held_sems.at[t]).wait()
    columns = fade_ref[...]
    lanes = lane_ids((ROWS, ROWS))
    squares = jnp.zeros((ROWS, ROWS), F32)
    for t in range(TILES):
        carried = lax.dot_general(c_ref[t], held_ref[t], NT, preferred_element_type=F32)
        total = within_ref[t] + spread_heads(columns, t) * carried
        gated = total.astype(BF16).astype(F32) * silu_ref[t]
        gated_ref[t] = gated
        squares = jnp.where(lanes == t, jnp.sum(gated * gated, axis=1, keepdims=True), squares)
    turned = jnp.transpose(squares)[:TILES]
    for i in range(squares_ref.shape[0]):
        squares_ref[i] = turned
    outs = [
        pltpu.make_async_copy(squares_ref, squares_hbm, out_sems.at[0]),
        pltpu.make_async_copy(gated_ref, gated_hbm, out_sems.at[1]),
    ]
    for out in outs:
        out.start()
    for out in outs:
        out.wait()


def norm_kernel(gated_hbm, squares_hbm, gain_hbm, out_hbm, *rest):
    gated_ref, squares_ref, gain_ref, out_ref, load_sems, sems = rest
    half = TILES // 2
    moves = [(squares_hbm, squares_ref), (gain_hbm, gain_ref)]
    for j in range(2):
        part = pl.ds(j * half, half)
        moves.append((gated_hbm.at[part], gated_ref.at[part]))
    loads = [pltpu.make_async_copy(*move, load_sems.at[i]) for i, move in enumerate(moves)]
    for load in loads:
        load.start()
    for load in loads[:2]:
        load.wait()
    total = jnp.sum(squares_ref[...], axis=0)
    factor = lax.rsqrt(total / NORM_WIDTH + 1e-05)
    filled = jnp.concatenate([factor, jnp.zeros((ROWS - TILES, ROWS), F32)], axis=0)
    columns = jnp.transpose(filled)
    gain = gain_ref[...]
    copies = []
    for j in range(2):
        loads[2 + j].wait()
        for t in range(j * half, (j + 1) * half):
            out_ref[t] = (gated_ref[t] * columns[:, t : t + 1] * gain).astype(BF16)
        part = pl.ds(j * half, half)
        copies.append(pltpu.make_async_copy(out_ref.at[part], out_hbm.at[part], sems.at[j]))
        copies[-1].start()
    for copy in copies:
        copy.wait()


def state_kernel(dest_hbm, states_hbm, got, *rest):
    fixed, second, out_hbm, rest = rest[:3], rest[3:7], rest[7], rest[8:]
    dest_ref, states_ref, held_ref, out_ref, used, sender, rank, sems, held_sems, out_sems = rest
    loads = [
        pltpu.make_async_copy(dest_hbm, dest_ref, sems.at[0]),
        pltpu.make_async_copy(states_hbm, states_ref, sems.at[1]),
    ]
    for load in loads:
        load.start()
    loads[0].wait()
    route(dest_ref, used, sender, rank)
    me = lax.axis_index("dp")
    copies = []
    for i, (k, turn) in enumerate(FIXED):
        slot = rank[side_offsets(k, turn)[1]]
        copies.append((None, fixed[i], held_ref.at[slot], slot))
    for n, k in enumerate(doubles(used)):
        for turn in (0, 1):
            slot = rank[side_offsets(k, turn)[1]]
            copies.append((k > 0, second[2 * n + turn], held_ref.at[slot], slot))
    for origin in range(PLACES):
        o = lax.rem(me - origin + PLACES, PLACES)
        needed = (used[o] == 1) & ((used[against(o)] == 0) | (o == 0))
        copies.append((needed, got.at[origin], held_ref.at[rank[o]], rank[o]))
    act(copies, held_sems, True)
    loads[1].wait()
    outs = []
    for t in range(TILES):
        pltpu.make_async_copy(got.at[0], held_ref.at[t], held_sems.at[t]).wait()
        tail = held_ref[t, pl.ds(WIDTH, TAIL), :].astype(F32)
        for h in range(HEADS_DEV):
            rows = pl.ds(h * HEAD_DIM, HEAD_DIM)
            fade = tail[h : h + 1] + tail[HEADS_DEV + h : HEADS_DEV + h + 1]
            out_ref[t, rows, :] = (
                fade * states_ref[t, rows, :].astype(F32) + held_ref[t, rows, :].astype(F32)
            ).astype(BF16)
        outs.append(pltpu.make_async_copy(out_ref.at[t], out_hbm.at[t], out_sems.at[t]))
        outs[-1].start()
    for out in outs:
        out.wait()


def shifted(message, k, turn):
    pairs = []
    for g in range(PLACES):
        forth = k if k == 8 or g % 2 == turn else PLACES - k
        pairs.append((g, (g + forth) % PLACES))
    return lax.ppermute(message, "dp", pairs)


def exchange_second(k, second):
    if k == 0:
        return tuple(jnp.zeros((MESSAGE, STATE), BF16) for _ in (0, 1))
    return tuple(shifted(second[turn], k, turn) for turn in (0, 1))


def finish(first_pair, code, sent, arrays):
    x_in, z_in, b_in, c_in, dt_raw, a_log, d_skip, gain_row, state_rows, dest = arrays
    send, sent_fixed, sent_second = sent[0], sent[1:4], tuple(sent[4:8])
    group_size = lax.axis_size("tensor") // GROUPS
    tile_shape = (TILES, ROWS, WIDTH)
    state_scratch = pltpu.VMEM(state_rows.shape, BF16)
    message_scratch = pltpu.VMEM((TILES, MESSAGE, STATE), BF16)
    wide_scratch = pltpu.VMEM(tile_shape, F32)
    rows_scratch = pltpu.VMEM((TILES * HEADS_DEV, ROWS), F32)
    tile_scratch = pltpu.VMEM(tile_shape, BF16)
    dt_scratch = pltpu.VMEM(dt_raw.shape, F32)
    dma = pltpu.SemaphoreType.DMA

    fixed = [shifted(value, k, turn) for value, (k, turn) in zip(sent_fixed, FIXED)]
    got = lax.all_to_all(send, "dp", split_axis=0, concat_axis=0, tiled=True)

    local = pl.pallas_call(
        within_kernel,
        in_specs=[HBM] * 7,
        out_specs=[VMEM] * 3,
        out_shape=[
            jax.ShapeDtypeStruct(tile_shape, F32),
            jax.ShapeDtypeStruct((ROWS, TILES * HEADS_DEV), F32),
            jax.ShapeDtypeStruct(tile_shape, F32),
        ],
        scratch_shapes=[
            HEAD_NUMBERS,
            HEAD_NUMBERS,
            tile_scratch,
            tile_scratch,
            tile_scratch,
            tile_scratch,
            dt_scratch,
            rows_scratch,
            dma((7,)),
        ],
        compiler_params=params(),
        name="within",
    )(a_log, d_skip, x_in, b_in, c_in, z_in, dt_raw)

    if first_pair:
        second = exchange_second(first_pair, sent_second[:2])
        rest = (0,) + tuple(k for k in PAIRS if k > first_pair)
        branches = [functools.partial(exchange_second, k) for k in rest]
        inner = jnp.where(code > 0, code - first_pair + 1, 0)
        sent_second, local = lax.optimization_barrier((sent_second, local))
        later = lax.switch(inner, branches, sent_second[2:])
        local, later = lax.optimization_barrier((local, later))
        second += later
    else:
        second = sent_second
    within, fade, silu = local

    gated, squares = pl.pallas_call(
        gate_kernel,
        in_specs=[HBM] * 6 + [ANY],
        out_specs=[HBM] * 2,
        out_shape=[
            jax.ShapeDtypeStruct(tile_shape, F32),
            jax.ShapeDtypeStruct((group_size, TILES, ROWS), F32),
        ],
        scratch_shapes=[
            TILE_NUMBERS,
            tile_scratch,
            wide_scratch,
            wide_scratch,
            pltpu.VMEM((ROWS, TILES * HEADS_DEV), F32),
            state_scratch,
            wide_scratch,
            pltpu.VMEM((group_size, TILES, ROWS), F32),
            *TABLES,
            dma((5,)),
            dma((TILES,)),
            dma((2,)),
        ],
        compiler_params=params(4500000),
        name="gate",
    )(dest, c_in, silu, within, fade, state_rows, got)

    members = [list(range(g * group_size, (g + 1) * group_size)) for g in range(GROUPS)]
    all_squares = lax.all_to_all(
        squares, "tensor", split_axis=0, concat_axis=0, axis_index_groups=members, tiled=True
    )

    new_states = pl.pallas_call(
        state_kernel,
        in_specs=[HBM] * 2 + [ANY] * 8,
        out_specs=HBM,
        out_shape=jax.ShapeDtypeStruct(state_rows.shape, BF16),
        scratch_shapes=[
            TILE_NUMBERS,
            state_scratch,
            message_scratch,
            state_scratch,
            *TABLES,
            dma((2,)),
            dma((TILES,)),
            dma((TILES,)),
        ],
        compiler_params=params(4500000),
        name="new_states",
    )(dest, state_rows, got, *fixed, *second)

    mixed = pl.pallas_call(
        norm_kernel,
        in_specs=[HBM, ANY, HBM],
        out_specs=HBM,
        out_shape=jax.ShapeDtypeStruct(tile_shape, BF16),
        scratch_shapes=[
            wide_scratch,
            pltpu.VMEM((group_size, TILES, ROWS), F32),
            pltpu.VMEM((1, WIDTH), F32),
            tile_scratch,
            dma((4,)),
            dma((2,)),
        ],
        compiler_params=params(400000),
        name="norm",
    )(gated, all_squares, gain_row)
    return (mixed, new_states)


def on_device(x_in, z_in, b_in, c_in, dt_raw, a_log, d_skip, norm_gain, states, dest, accepted):
    gain_row = norm_gain.reshape(1, WIDTH)
    state_rows = states.reshape(TILES, WIDTH, STATE)
    tile_shape = (TILES, ROWS, WIDTH)
    message = jax.ShapeDtypeStruct((MESSAGE, STATE), BF16)
    messages = jax.ShapeDtypeStruct((PLACES, MESSAGE, STATE), BF16)
    state_scratch = pltpu.VMEM(state_rows.shape, BF16)
    message_scratch = pltpu.VMEM((TILES, MESSAGE, STATE), BF16)
    rows_scratch = pltpu.VMEM((TILES * HEADS_DEV, ROWS), F32)
    tile_scratch = pltpu.VMEM(tile_shape, BF16)
    dt_scratch = pltpu.VMEM(dt_raw.shape, F32)
    dma = pltpu.SemaphoreType.DMA

    sent = pl.pallas_call(
        added_kernel,
        in_specs=[HBM] * 7,
        out_specs=[HBM] * 8 + [pl.BlockSpec(memory_space=pltpu.SMEM)] * 2,
        out_shape=[messages] + [message] * 7 + [jax.ShapeDtypeStruct((1,), jnp.int32)] * 2,
        scratch_shapes=[
            TILE_NUMBERS,
            TILE_NUMBERS,
            HEAD_NUMBERS,
            tile_scratch,
            tile_scratch,
            dt_scratch,
            rows_scratch,
            state_scratch,
            message_scratch,
            *TABLES,
            dma((7,)),
            dma((PLACES + 7,)),
        ],
        compiler_params=params(),
        name="added",
    )(dest, accepted, a_log, x_in, b_in, dt_raw, state_rows)
    *sent, first_code, second_code = sent
    arrays = (x_in, z_in, b_in, c_in, dt_raw, a_log, d_skip, gain_row, state_rows, dest)
    branches = [functools.partial(finish, k) for k in (0,) + PAIRS]
    mixed, new_states = lax.switch(
        first_code.reshape(()), branches, second_code.reshape(()), sent, arrays
    )
    return (mixed, new_states.reshape(states.shape))


def solution(mesh):
    in_specs = (
        P("dp", None, "tensor"),
        P("dp", None, "tensor"),
        P("dp", None, None),
        P("dp", None, None),
        P("dp", "tensor", None),
        P("tensor"),
        P("tensor"),
        P("tensor"),
        P("dp", "tensor", None, None),
        P(),
        P(),
    )
    out_specs = (P("dp", None, "tensor"), P("dp", "tensor", None, None))
    return jax.shard_map(
        on_device, mesh=mesh, in_specs=in_specs, out_specs=out_specs, check_vma=False
    )
```

```python
import functools

import jax
import jax.numpy as jnp
from jax import lax
from jax.experimental import pallas as pl
from jax.experimental.pallas import tpu as pltpu
from jax.sharding import PartitionSpec as P

GROUPS = 4
PLACES = 16
TILES = 8
HEADS_DEV = 4
HEAD_DIM = 64
STATE = 256
ROWS = 128
WIDTH = HEADS_DEV * HEAD_DIM
TAIL = 16
MESSAGE = WIDTH + TAIL
NORM_WIDTH = 2048.0
FIXED = ((8, 0), (1, 0), (1, 1))
PAIRS = (2, 3, 4, 5, 6, 7)
VMEM_BYTES = 63471616
F32 = jnp.float32
BF16 = jnp.bfloat16
ANY = pl.BlockSpec(memory_space=pl.ANY)
HBM = pl.BlockSpec(memory_space=pltpu.HBM)
VMEM = pl.BlockSpec(memory_space=pltpu.VMEM)
NN = (((1,), (0,)), ((), ()))
NT = (((1,), (1,)), ((), ()))
TN = (((0,), (0,)), ((), ()))
TABLES = [pltpu.SMEM((PLACES,), jnp.int32)] * 3
TILE_NUMBERS = pltpu.SMEM((PLACES * TILES,), jnp.int32)
HEAD_NUMBERS = pltpu.SMEM((HEADS_DEV,), F32)


def params(room=0):
    return pltpu.CompilerParams(vmem_limit_bytes=VMEM_BYTES - room)


def lane_ids(shape):
    return lax.broadcasted_iota(jnp.int32, shape, len(shape) - 1)


def route(dest_ref, used, sender, rank):
    me = lax.axis_index("dp")
    for o in range(PLACES):
        used[o] = 0
        sender[o] = 0
    for t in range(TILES):
        used[dest_ref[t]] = 1
        sender[lax.rem(dest_ref[me * TILES + t] - me + PLACES, PLACES)] = t
    count = 0
    for g in range(PLACES):
        o = lax.rem(me - g + PLACES, PLACES)
        rank[o] = count
        count = count + used[o]


def side_offsets(k, turn):
    if isinstance(k, int) and k == 8:
        return 8, 8
    mine = jnp.where(lax.rem(lax.axis_index("dp"), 2) == turn, k, PLACES - k)
    return mine, jnp.where(lax.rem(k, 2) == 0, mine, PLACES - mine)


def doubles(used):
    found = [jnp.int32(0), jnp.int32(0)]
    count = jnp.int32(0)
    for k in PAIRS:
        both = used[k] * used[PLACES - k]
        for n in range(2):
            found[n] = jnp.where((both == 1) & (count == n), k, found[n])
        count = count + both
    return found


def against(o):
    return lax.rem(PLACES - o, PLACES)


def step_rows(dt_ref, a_ref, rows_ref):
    for t in range(TILES):
        rows_ref[pl.ds(t * HEADS_DEV, HEADS_DEV), :] = dt_ref[t]
    raw = rows_ref[...]
    step = jnp.maximum(raw, 0.0) + jnp.log1p(jnp.exp(-jnp.abs(raw)))
    head = lax.rem(lax.broadcasted_iota(jnp.int32, raw.shape, 0), HEADS_DEV)
    a_log = jnp.zeros(raw.shape, F32)
    for h in range(HEADS_DEV):
        a_log = jnp.where(head == h, a_ref[h], a_log)
    total = -jnp.exp(a_log) * step
    lanes = lane_ids(total.shape)
    shift = 1
    while shift < ROWS:
        total = total + jnp.where(lanes >= shift, pltpu.roll(total, shift, 1), 0.0)
        shift *= 2
    return step, total


def spread_heads(columns, t):
    low = lane_ids((ROWS, 2 * HEAD_DIM)) < HEAD_DIM
    halves = []
    for j in range(2):
        at = t * HEADS_DEV + 2 * j
        halves.append(jnp.where(low, columns[:, at : at + 1], columns[:, at + 1 : at + 2]))
    return jnp.concatenate(halves, axis=1)


def group_part(ref):
    size = lax.axis_size("tensor") // GROUPS
    first = lax.div(lax.axis_index("tensor"), size) * STATE
    return ref.at[:, :, pl.ds(pl.multiple_of(first, STATE), STATE)]


def act(copies, sems, start):
    for needed, source, target, sem in copies:
        copy = pltpu.make_async_copy(source, target, sems.at[sem])
        step = copy.start if start else copy.wait
        if needed is None:
            step()
        else:
            pl.when(needed)(step)


def added_kernel(dest_hbm, accepted_hbm, a_hbm, x_hbm, b_hbm, dt_hbm, states_hbm, *rest):
    send, fixed, second = rest[0], rest[1:4], rest[4:8]
    dest_ref, accepted_ref, a_ref, x_ref, b_ref, dt_ref, rows_ref, states_ref = rest[8:16]
    added_ref, used, sender, rank, sems, out_sems = rest[16:]
    moves = (
        (dest_hbm, dest_ref),
        (accepted_hbm, accepted_ref),
        (a_hbm, a_ref),
        (dt_hbm, dt_ref),
        (states_hbm, states_ref),
        (x_hbm, x_ref),
        (group_part(b_hbm), b_ref),
    )
    loads = [pltpu.make_async_copy(*move, sems.at[i]) for i, move in enumerate(moves)]
    for load in loads:
        load.start()
    for load in loads[:4]:
        load.wait()
    route(dest_ref, used, sender, rank)
    me = lax.axis_index("dp")
    part = pl.ds(0, WIDTH)
    early = []
    for to in range(PLACES):
        o = lax.rem(to - me + PLACES, PLACES)
        needed = (used[against(o)] == 1) & (o != 0)
        early.append((needed, states_ref.at[rank[against(o)]], send.at[to, part, :], to))
    step, total = step_rows(dt_ref, a_ref, rows_ref)
    shape = total.shape
    lanes = lane_ids(shape)
    row_tile = lax.div(lax.broadcasted_iota(jnp.int32, shape, 0), HEADS_DEV)
    accepted = jnp.zeros(shape, jnp.int32)
    for t in range(TILES):
        accepted = jnp.where(row_tile == t, accepted_ref[me * TILES + t], accepted)
    final = jnp.sum(jnp.where(lanes == accepted - 1, total, 0.0), axis=1, keepdims=True)
    kept = lanes < accepted
    scale = jnp.where(kept, jnp.exp(jnp.where(kept, final - total, 0.0)), 0.0) * step
    columns = jnp.transpose(scale)
    fade = jnp.broadcast_to(jnp.exp(final), (shape[0], STATE))
    fade_high = fade.astype(BF16).astype(F32)
    fade_low = fade - fade_high
    empty = jnp.zeros((TAIL - 2 * HEADS_DEV, STATE), F32)
    loads[4].wait()
    act(early, out_sems, True)
    for load in loads[5:]:
        load.wait()
    late = []
    for t in range(TILES):
        x_kept = (x_ref[t].astype(F32) * spread_heads(columns, t)).astype(BF16)
        added = lax.dot_general(x_kept, b_ref[t], TN, preferred_element_type=F32)
        added_ref[t, part, :] = added.astype(BF16)
        at = t * HEADS_DEV
        tail = jnp.concatenate(
            [fade_high[at : at + HEADS_DEV], fade_low[at : at + HEADS_DEV], empty], axis=0
        )
        added_ref[t, pl.ds(WIDTH, TAIL), :] = tail.astype(BF16)
        to = dest_ref[me * TILES + t]
        o = lax.rem(to - me + PLACES, PLACES)
        late.append(((used[against(o)] == 0) | (o == 0), added_ref.at[t], send.at[to], to))
        act(late[-1:], out_sems, True)
    seconds = []
    for i, (k, turn) in enumerate(FIXED):
        o = side_offsets(k, turn)[0]
        seconds.append((None, added_ref.at[sender[o]], fixed[i], PLACES + i))
    for n, k in enumerate(doubles(used)):
        for turn in (0, 1):
            o = side_offsets(k, turn)[0]
            i = 2 * n + turn
            seconds.append((k > 0, added_ref.at[sender[o]], second[i], PLACES + 3 + i))
    act(seconds, out_sems, True)
    late += seconds
    act(early, out_sems, False)
    act(late, out_sems, False)


def within_kernel(a_hbm, d_hbm, x_hbm, b_hbm, c_hbm, z_hbm, dt_hbm, *rest):
    out_ref, fade_ref, silu_ref, a_ref, d_ref, c_ref, x_ref, b_ref, z_ref, dt_ref = rest[:10]
    rows_ref, sems = rest[10:]
    moves = (
        (a_hbm, a_ref),
        (d_hbm, d_ref),
        (dt_hbm, dt_ref),
        (z_hbm, z_ref),
        (group_part(c_hbm), c_ref),
        (group_part(b_hbm), b_ref),
        (x_hbm, x_ref),
    )
    loads = [pltpu.make_async_copy(*move, sems.at[i]) for i, move in enumerate(moves)]
    for load in loads:
        load.start()
    for load in loads[:3]:
        load.wait()
    step, total = step_rows(dt_ref, a_ref, rows_ref)
    columns = jnp.transpose(total)
    fade_ref[...] = jnp.exp(columns)
    lower = lane_ids((ROWS, ROWS)) <= lax.broadcasted_iota(jnp.int32, (ROWS, ROWS), 0)
    wide = lax.div(lane_ids((ROWS, WIDTH)), HEAD_DIM)
    head = lax.div(lane_ids((1, WIDTH)), HEAD_DIM)
    skip = jnp.zeros((1, WIDTH), F32)
    for h in range(HEADS_DEV):
        skip = jnp.where(head == h, d_ref[h], skip)
    for load in loads[3:]:
        load.wait()
    for t in range(TILES):
        z = z_ref[t].astype(F32)
        silu_ref[t] = z / (1.0 + jnp.exp(-z))
        products = lax.dot_general(c_ref[t], b_ref[t], NT, preferred_element_type=F32)
        x = x_ref[t]
        weights = []
        inputs = []
        for h in range(HEADS_DEV):
            at = t * HEADS_DEV + h
            gap = columns[:, at : at + 1] - total[at : at + 1, :]
            decay = jnp.exp(jnp.where(lower, gap, -1e30))
            weights.append((products * decay * step[at : at + 1, :]).astype(BF16))
            inputs.append(jnp.where(wide == h, x, jnp.zeros_like(x)))
        within = lax.dot_general(
            jnp.concatenate(weights, axis=1),
            jnp.concatenate(inputs, axis=0),
            NN,
            preferred_element_type=F32,
        )
        out_ref[t] = within + skip * x.astype(F32)


def gate_kernel(dest_hbm, c_hbm, silu_hbm, within_hbm, fade_hbm, states_hbm, got, *rest):
    gated_hbm, squares_hbm = rest[:2]
    dest_ref, c_ref, silu_ref, within_ref, fade_ref, held_ref, gated_ref = rest[2:9]
    squares_ref, used, sender, rank, sems, held_sems, out_sems = rest[9:]
    moves = (
        (dest_hbm, dest_ref),
        (fade_hbm, fade_ref),
        (group_part(c_hbm), c_ref),
        (within_hbm, within_ref),
        (silu_hbm, silu_ref),
    )
    loads = [pltpu.make_async_copy(*move, sems.at[i]) for i, move in enumerate(moves)]
    for load in loads:
        load.start()
    loads[0].wait()
    route(dest_ref, used, sender, rank)
    part = pl.ds(0, WIDTH)
    me = lax.axis_index("dp")
    copies = [(used[0] == 1, states_hbm.at[rank[0]], sender[0])]
    for origin in range(PLACES):
        o = lax.rem(me - origin + PLACES, PLACES)
        needed = (used[against(o)] == 1) & (o != 0)
        copies.append((needed, got.at[origin, part, :], sender[against(o)]))
    copies = [(needed, source, held_ref.at[t], t) for needed, source, t in copies]
    act(copies, held_sems, True)
    for load in loads[1:]:
        load.wait()
    for t in range(TILES):
        pltpu.make_async_copy(states_hbm.at[0], held_ref.at[t], held_sems.at[t]).wait()
    columns = fade_ref[...]
    lanes = lane_ids((ROWS, ROWS))
    squares = jnp.zeros((ROWS, ROWS), F32)
    for t in range(TILES):
        carried = lax.dot_general(c_ref[t], held_ref[t], NT, preferred_element_type=F32)
        total = within_ref[t] + spread_heads(columns, t) * carried
        gated = total.astype(BF16).astype(F32) * silu_ref[t]
        gated_ref[t] = gated
        squares = jnp.where(lanes == t, jnp.sum(gated * gated, axis=1, keepdims=True), squares)
    turned = jnp.transpose(squares)[:TILES]
    for i in range(squares_ref.shape[0]):
        squares_ref[i] = turned
    outs = [
        pltpu.make_async_copy(squares_ref, squares_hbm, out_sems.at[0]),
        pltpu.make_async_copy(gated_ref, gated_hbm, out_sems.at[1]),
    ]
    for out in outs:
        out.start()
    for out in outs:
        out.wait()


def norm_kernel(gated_hbm, squares_hbm, gain_hbm, out_hbm, *rest):
    gated_ref, squares_ref, gain_ref, out_ref, load_sems, sems = rest
    half = TILES // 2
    moves = [(squares_hbm, squares_ref), (gain_hbm, gain_ref)]
    for j in range(2):
        part = pl.ds(j * half, half)
        moves.append((gated_hbm.at[part], gated_ref.at[part]))
    loads = [pltpu.make_async_copy(*move, load_sems.at[i]) for i, move in enumerate(moves)]
    for load in loads:
        load.start()
    for load in loads[:2]:
        load.wait()
    total = jnp.sum(squares_ref[...], axis=0)
    factor = lax.rsqrt(total / NORM_WIDTH + 1e-05)
    filled = jnp.concatenate([factor, jnp.zeros((ROWS - TILES, ROWS), F32)], axis=0)
    columns = jnp.transpose(filled)
    gain = gain_ref[...]
    copies = []
    for j in range(2):
        loads[2 + j].wait()
        for t in range(j * half, (j + 1) * half):
            out_ref[t] = (gated_ref[t] * columns[:, t : t + 1] * gain).astype(BF16)
        part = pl.ds(j * half, half)
        copies.append(pltpu.make_async_copy(out_ref.at[part], out_hbm.at[part], sems.at[j]))
        copies[-1].start()
    for copy in copies:
        copy.wait()


def state_kernel(dest_hbm, states_hbm, got, *rest):
    fixed, second, out_hbm, rest = rest[:3], rest[3:7], rest[7], rest[8:]
    dest_ref, states_ref, held_ref, out_ref, used, sender, rank, sems, held_sems, out_sems = rest
    loads = [
        pltpu.make_async_copy(dest_hbm, dest_ref, sems.at[0]),
        pltpu.make_async_copy(states_hbm, states_ref, sems.at[1]),
    ]
    for load in loads:
        load.start()
    loads[0].wait()
    route(dest_ref, used, sender, rank)
    me = lax.axis_index("dp")
    copies = []
    for i, (k, turn) in enumerate(FIXED):
        slot = rank[side_offsets(k, turn)[1]]
        copies.append((None, fixed[i], held_ref.at[slot], slot))
    for n, k in enumerate(doubles(used)):
        for turn in (0, 1):
            slot = rank[side_offsets(k, turn)[1]]
            copies.append((k > 0, second[2 * n + turn], held_ref.at[slot], slot))
    for origin in range(PLACES):
        o = lax.rem(me - origin + PLACES, PLACES)
        needed = (used[o] == 1) & ((used[against(o)] == 0) | (o == 0))
        copies.append((needed, got.at[origin], held_ref.at[rank[o]], rank[o]))
    act(copies, held_sems, True)
    loads[1].wait()
    outs = []
    for t in range(TILES):
        pltpu.make_async_copy(got.at[0], held_ref.at[t], held_sems.at[t]).wait()
        tail = held_ref[t, pl.ds(WIDTH, TAIL), :].astype(F32)
        for h in range(HEADS_DEV):
            rows = pl.ds(h * HEAD_DIM, HEAD_DIM)
            fade = tail[h : h + 1] + tail[HEADS_DEV + h : HEADS_DEV + h + 1]
            out_ref[t, rows, :] = (
                fade * states_ref[t, rows, :].astype(F32) + held_ref[t, rows, :].astype(F32)
            ).astype(BF16)
        outs.append(pltpu.make_async_copy(out_ref.at[t], out_hbm.at[t], out_sems.at[t]))
        outs[-1].start()
    for out in outs:
        out.wait()


def shifted(message, k, turn):
    pairs = []
    for g in range(PLACES):
        forth = k if k == 8 or g % 2 == turn else PLACES - k
        pairs.append((g, (g + forth) % PLACES))
    return lax.ppermute(message, "dp", pairs)


def exchange_second(k, second):
    if k == 0:
        return tuple(jnp.zeros((MESSAGE, STATE), BF16) for _ in (0, 1))
    return tuple(shifted(second[turn], k, turn) for turn in (0, 1))


def on_device(x_in, z_in, b_in, c_in, dt_raw, a_log, d_skip, norm_gain, states, dest, accepted):
    group_size = lax.axis_size("tensor") // GROUPS
    gain_row = norm_gain.reshape(1, WIDTH)
    state_rows = states.reshape(TILES, WIDTH, STATE)
    tile_shape = (TILES, ROWS, WIDTH)
    message = jax.ShapeDtypeStruct((MESSAGE, STATE), BF16)
    messages = jax.ShapeDtypeStruct((PLACES, MESSAGE, STATE), BF16)
    state_scratch = pltpu.VMEM(state_rows.shape, BF16)
    message_scratch = pltpu.VMEM((TILES, MESSAGE, STATE), BF16)
    wide_scratch = pltpu.VMEM(tile_shape, F32)
    rows_scratch = pltpu.VMEM((TILES * HEADS_DEV, ROWS), F32)
    tile_scratch = pltpu.VMEM(tile_shape, BF16)
    dt_scratch = pltpu.VMEM(dt_raw.shape, F32)
    dma = pltpu.SemaphoreType.DMA

    pairs = jnp.array(PAIRS, jnp.int32)[:, None]
    hits = jnp.sum((dest[None, :TILES] == pairs) | (dest[None, :TILES] == PLACES - pairs), axis=1)
    both = hits == 2
    order = jnp.arange(len(PAIRS), dtype=jnp.int32)
    earlier = jnp.sum(both[None, :] & (order[None, :] < order[:, None]), axis=1)
    second_codes = [jnp.sum(jnp.where(both & (earlier == n), order + 1, 0)) for n in range(2)]

    sent = pl.pallas_call(
        added_kernel,
        in_specs=[HBM] * 7,
        out_specs=[HBM] * 8,
        out_shape=[messages] + [message] * 7,
        scratch_shapes=[
            TILE_NUMBERS,
            TILE_NUMBERS,
            HEAD_NUMBERS,
            tile_scratch,
            tile_scratch,
            dt_scratch,
            rows_scratch,
            state_scratch,
            message_scratch,
            *TABLES,
            dma((7,)),
            dma((PLACES + 7,)),
        ],
        compiler_params=params(),
        name="added",
    )(dest, accepted, a_log, x_in, b_in, dt_raw, state_rows)
    send, sent_fixed, sent_second = sent[0], sent[1:4], sent[4:8]

    fixed = [shifted(value, k, turn) for value, (k, turn) in zip(sent_fixed, FIXED)]
    got = lax.all_to_all(send, "dp", split_axis=0, concat_axis=0, tiled=True)

    local = pl.pallas_call(
        within_kernel,
        in_specs=[HBM] * 7,
        out_specs=[VMEM] * 3,
        out_shape=[
            jax.ShapeDtypeStruct(tile_shape, F32),
            jax.ShapeDtypeStruct((ROWS, TILES * HEADS_DEV), F32),
            jax.ShapeDtypeStruct(tile_shape, F32),
        ],
        scratch_shapes=[
            HEAD_NUMBERS,
            HEAD_NUMBERS,
            tile_scratch,
            tile_scratch,
            tile_scratch,
            tile_scratch,
            dt_scratch,
            rows_scratch,
            dma((7,)),
        ],
        compiler_params=params(),
        name="within",
    )(a_log, d_skip, x_in, b_in, c_in, z_in, dt_raw)

    local, sent_second, second_codes = lax.optimization_barrier((local, sent_second, second_codes))
    within, fade, silu = local
    branches = [functools.partial(exchange_second, k) for k in (0,) + PAIRS]
    later = lax.switch(second_codes[1], branches, sent_second[2:])
    later, sent_second, within = lax.optimization_barrier((later, sent_second, within))

    gate = pl.pallas_call(
        gate_kernel,
        in_specs=[HBM] * 6 + [ANY],
        out_specs=[HBM] * 2,
        out_shape=[
            jax.ShapeDtypeStruct(tile_shape, F32),
            jax.ShapeDtypeStruct((group_size, TILES, ROWS), F32),
        ],
        scratch_shapes=[
            TILE_NUMBERS,
            tile_scratch,
            wide_scratch,
            wide_scratch,
            pltpu.VMEM((ROWS, TILES * HEADS_DEV), F32),
            state_scratch,
            wide_scratch,
            pltpu.VMEM((group_size, TILES, ROWS), F32),
            *TABLES,
            dma((5,)),
            dma((TILES,)),
            dma((2,)),
        ],
        compiler_params=params(4500000),
        name="gate",
    )

    def exchange_and_gate(k, values, operands):
        return exchange_second(k, values), gate(*operands)

    branches = [functools.partial(exchange_and_gate, k) for k in (0,) + PAIRS]
    operands = (dest, c_in, silu, within, fade, state_rows, got)
    second, (gated, squares) = lax.switch(
        second_codes[0], branches, sent_second[:2], operands
    )
    second += later

    members = [list(range(g * group_size, (g + 1) * group_size)) for g in range(GROUPS)]
    all_squares = lax.all_to_all(
        squares, "tensor", split_axis=0, concat_axis=0, axis_index_groups=members, tiled=True
    )

    new_states = pl.pallas_call(
        state_kernel,
        in_specs=[HBM] * 2 + [ANY] * 8,
        out_specs=HBM,
        out_shape=jax.ShapeDtypeStruct(state_rows.shape, BF16),
        scratch_shapes=[
            TILE_NUMBERS,
            state_scratch,
            message_scratch,
            state_scratch,
            *TABLES,
            dma((2,)),
            dma((TILES,)),
            dma((TILES,)),
        ],
        compiler_params=params(4500000),
        name="new_states",
    )(dest, state_rows, got, *fixed, *second)

    mixed = pl.pallas_call(
        norm_kernel,
        in_specs=[HBM, ANY, HBM],
        out_specs=HBM,
        out_shape=jax.ShapeDtypeStruct(tile_shape, BF16),
        scratch_shapes=[
            wide_scratch,
            pltpu.VMEM((group_size, TILES, ROWS), F32),
            pltpu.VMEM((1, WIDTH), F32),
            tile_scratch,
            dma((4,)),
            dma((2,)),
        ],
        compiler_params=params(400000),
        name="norm",
    )(gated, all_squares, gain_row)
    return (mixed, new_states.reshape(states.shape))


def solution(mesh):
    in_specs = (
        P("dp", None, "tensor"),
        P("dp", None, "tensor"),
        P("dp", None, None),
        P("dp", None, None),
        P("dp", "tensor", None),
        P("tensor"),
        P("tensor"),
        P("tensor"),
        P("dp", "tensor", None, None),
        P(),
        P(),
    )
    out_specs = (P("dp", None, "tensor"), P("dp", "tensor", None, None))
    return jax.shard_map(
        on_device, mesh=mesh, in_specs=in_specs, out_specs=out_specs, check_vma=False
    )
```
